32 devices in a mesh: row: 8 (over z, y), col: 4 (over x, core).
Axes of the slice: x: 2, y: 2, z: 4, core: 2. Of those that a mesh axis runs over, the one named last changes fastest.
Arguments:
- object_field: float32 [2, 1024, 512], P(None, 'row', 'col'), may hold values from -4.2 to 4.2
- probe: float32 [2, 128, 128], replicated, may hold values from -8.4 to 8.4
- positions: int32 [8, 4, 2, 4, 2], P('row', 'col'), may hold values from -64 to 64
- counts: int32 [8, 4, 2], P('row', 'col'), may hold values from 1 to 4, as said below
- amplitude: float32 [8, 4, 2, 4, 128, 128], P('row', 'col'), may hold values from 0.5 to 4
Outputs:
- object_out: float32 [2, 1024, 512], P(None, 'row', 'col')
- probe_out: float32 [2, 128, 128], replicated
The draws below stay inside these ranges and needn't reach their ends.
Inputs may be any that keep to these rules, and one draw needn't show every extreme that they name: `counts`: some tile has all 4 slots live in some mini-batch.
All inputs are finite; a program needn't handle non-finite values.
Results may differ from the reference program's by a relative error of at most 0.00013.
Values sent between devices are 32-bit elements; how exact they have to be, the bound alone decides.
No kernel may reach another device: no remote copies, remote signals or barrier semaphores. Data moves between devices by JAX's collectives and lax.ppermute only.
A program may use at most 64 MiB of HBM per device.

```python
import math
import jax
import jax.numpy as jnp
from jax import lax

NPIX = 128
RIM = 64
TS = 128
SLOTS = 4
ITERS = 2
TILES_R = 8
TILES_C = 4
NY = 1024
NX = 512


def draw_counts(key, part):
    key = jax.random.fold_in(key, 7)
    first, second = jax.random.split(key)
    total = TILES_R * TILES_C * ITERS
    base = jax.random.randint(first, (total,), 1, SLOTS + 1)
    pick = jax.random.randint(second, (), 0, total)
    base = base.at[pick].set(SLOTS)
    return base.reshape(TILES_R, TILES_C, ITERS).astype(jnp.int32)


def with_ends(entries, rng, least, high):
    longest = entries.shape.index(max(entries.shape))
    spots = []
    for shift in (0, 1):
        where = [jax.random.randint(jax.random.fold_in(rng, axis), (), 0, length) for axis, length in enumerate(entries.shape)]
        where[longest] = (where[longest] + shift) % entries.shape[longest]
        spots.append(tuple(where))
    return entries.at[spots[0]].set(least).at[spots[1]].set(high)


def steps_of(rng, shape, cuts, smallest, high):
    gain = 1.0
    for dim, blocks in cuts:
        steps = jax.random.uniform(jax.random.fold_in(jax.random.fold_in(rng, 6), dim), (blocks,), jnp.float32, smallest / len(cuts), high / len(cuts))
        gain = gain * jnp.repeat(jnp.exp(steps), shape[dim] // blocks).reshape((-1,) + (1,) * (len(shape) - 1 - dim))
    return gain


def noise(rng, dims, spread, reach, cuts=(), kind=jnp.bfloat16):
    level = steps_of(rng, dims, cuts, -0.22, 0.18) if cuts else 1.0
    array = jax.random.normal(rng, dims, jnp.float32) * spread * level
    return jnp.minimum(jnp.maximum(array, -reach), reach).astype(kind)


def setup_inputs(seed: int = 0) -> dict:
    keys = jax.random.split(jax.random.key(seed), 6)
    return {
        "object_field": noise(keys[0], (2, NY, NX), 0.7, 4.2, ((1, 8), (2, 4)), jnp.float32),
        "probe": noise(keys[1], (2, NPIX, NPIX), 1.4, 8.4, (), jnp.float32),
        "positions": with_ends(jax.random.randint(keys[2], (TILES_R, TILES_C, ITERS, SLOTS, 2), 0 - RIM, TS - RIM + 1), jax.random.fold_in(keys[2], 1), 0 - RIM, TS - RIM).astype(jnp.int32),
        "counts": draw_counts(jax.random.fold_in(keys[5], 71), 0),
        "amplitude": jnp.clip(jnp.exp(math.log(4.0) - 2.0794415 * jax.random.uniform(keys[4], (TILES_R, TILES_C, ITERS, SLOTS, NPIX, NPIX), jnp.float32) ** steps_of(keys[4], (TILES_R, TILES_C, ITERS, SLOTS, NPIX, NPIX), ((0, 8), (1, 4)), -0.2, 0.2)), 0.5, 4.0),
    }


def reference(object_field, probe, positions, counts, amplitude):
    obj = object_field[0] + 1j * object_field[1]
    prb = probe[0] + 1j * probe[1]
    tile_r = (jnp.arange(TILES_R, dtype=jnp.int32) * TS)[:, None, None, None]
    tile_c = (jnp.arange(TILES_C, dtype=jnp.int32) * TS)[None, :, None, None]
    glob_y = (positions[..., 0] + tile_r + RIM).astype(jnp.int32)
    glob_x = (positions[..., 1] + tile_c + RIM).astype(jnp.int32)
    slot_ids = jnp.arange(SLOTS, dtype=jnp.int32)[None, None, None, :]
    live = (slot_ids < counts[..., None]).astype(jnp.float32)
    for step in range(ITERS):
        padded = jnp.pad(obj, RIM)
        ys = glob_y[:, :, step].reshape(-1)
        xs = glob_x[:, :, step].reshape(-1)
        lv = live[:, :, step].reshape(-1)
        amps = amplitude[:, :, step].reshape(-1, NPIX, NPIX)

        def advance(carry, item):
            num, den, pnum, pden = carry
            y, x, flag, amp = item
            win = lax.dynamic_slice(padded, (y, x), (NPIX, NPIX))
            psi = prb * win
            far = jnp.fft.fft2(psi, norm="ortho")
            factor = amp / jnp.maximum(jnp.abs(far), 1.0)
            chi = (jnp.fft.ifft2(far * factor, norm="ortho") - psi) * flag
            old = lax.dynamic_slice(num, (y, x), (NPIX, NPIX))
            num = lax.dynamic_update_slice(num, old + jnp.conj(prb) * chi, (y, x))
            oldd = lax.dynamic_slice(den, (y, x), (NPIX, NPIX))
            den = lax.dynamic_update_slice(den, oldd + jnp.abs(prb) ** 2 * flag, (y, x))
            pnum = pnum + jnp.conj(win) * chi
            pden = pden + jnp.abs(win) ** 2 * flag
            return (num, den, pnum, pden), None

        init = (jnp.zeros(padded.shape, padded.dtype), jnp.zeros(padded.shape, jnp.float32),
                jnp.zeros((NPIX, NPIX), prb.dtype), jnp.zeros((NPIX, NPIX), jnp.float32))
        (num, den, pnum, pden), _ = lax.scan(advance, init, (ys, xs, lv, amps))
        num = num[RIM:RIM + NY, RIM:RIM + NX]
        den = den[RIM:RIM + NY, RIM:RIM + NX]
        obj = obj + num / (den + 0.1)
        prb = prb + pnum / (pden + 0.1)
    object_out = jnp.stack([jnp.real(obj), jnp.imag(obj)]).astype(jnp.float32)
    probe_out = jnp.stack([jnp.real(prb), jnp.imag(prb)]).astype(jnp.float32)
    return object_out, probe_out
```

```python
import functools
import math

import jax
import jax.numpy as jnp
import numpy as np
from jax import lax
from jax.experimental import pallas as pl
from jax.experimental.pallas import tpu as pltpu
from jax.sharding import PartitionSpec as P

RIM = 64
TILE = 8
AXES = ("row", "col")


def dft_tables(size):
    index = np.arange(size)
    angle = (index[:, None] * index[None, :] % size) * (-2.0 * math.pi / size)
    cosine = np.cos(angle) / math.sqrt(size)
    sine = np.sin(angle) / math.sqrt(size)
    full = np.block([[cosine, -sine], [sine, cosine]]).astype(np.float32)
    flip = np.ascontiguousarray(full.T)
    tables = []
    for table in (full, flip):
        high = table.astype(jnp.bfloat16)
        tables += [high, (table - high.astype(np.float32)).astype(jnp.bfloat16)]
    return np.stack(tables)


def split(value):
    high = value.astype(jnp.bfloat16)
    return high, (value - high.astype(jnp.float32)).astype(jnp.bfloat16)


def mul(left, right):
    return jnp.dot(left, right, preferred_element_type=jnp.float32)


def left_product(high, low, value):
    first, second = split(value)
    return mul(high, first) + (mul(high, second) + mul(low, first))


def right_product(value, high, low):
    first, second = split(value)
    return mul(first, high) + (mul(second, high) + mul(first, low))


def slots_kernel(starts, count, field, probe, amps, tables, sums, probe_sums):
    width = probe.shape[1]
    tiles = width // TILE
    lane = lax.broadcasted_iota(jnp.int32, (width + TILE, width), 1)
    sub = lax.broadcasted_iota(jnp.int32, (tiles, TILE, width), 1)
    sums[...] = jnp.zeros_like(sums)
    full_h, full_l, flip_h, flip_l = (tables[k] for k in range(4))
    pro_r, pro_i = probe[0], probe[1]
    weight = pro_r * pro_r + pro_i * pro_i
    total = None
    for slot in range(amps.shape[0]):
        row = starts[2 * slot] + RIM
        col = starts[2 * slot + 1]
        live = jnp.where(slot < count[0], 1.0, 0.0).astype(jnp.float32)
        base = pl.multiple_of(row // TILE * TILE, TILE)
        rows = pl.ds(base, width + TILE)
        skew = row - base
        lift = jnp.where(skew > 0, TILE - skew, 0)
        back = jnp.where(col > 0, width - col, -col)
        ahead = jnp.where(col < 0, width + col, col)
        outside = (lane < col) | (lane >= width + col)

        def window(part):
            mixed = jnp.where(outside, field[part, rows, width:], field[part, rows, :width])
            turned = pltpu.roll(mixed.reshape(tiles + 1, TILE, width), lift, 1)
            lined = jnp.where(sub < TILE - skew, turned[:-1], turned[1:])
            return pltpu.roll(lined.reshape(width, width), back, 1)

        win_r, win_i = window(0), window(1)
        psi_r = pro_r * win_r - pro_i * win_i
        psi_i = pro_r * win_i + pro_i * win_r
        half = left_product(full_h, full_l, jnp.concatenate([psi_r, psi_i], 0))
        far = right_product(jnp.concatenate([half[:width], half[width:]], 1), flip_h, flip_l)
        far_r, far_i = far[:, :width], far[:, width:]
        factor = amps[slot] * lax.rsqrt(jnp.maximum(far_r * far_r + far_i * far_i, 1.0))
        half = left_product(
            flip_h, flip_l, jnp.concatenate([far_r * factor, far_i * factor], 0)
        )
        back_ = right_product(jnp.concatenate([half[:width], half[width:]], 1), full_h, full_l)
        chi_r = (back_[:, :width] - psi_r) * live
        chi_i = (back_[:, width:] - psi_i) * live

        def deposit(part, term):
            moved = pltpu.roll(term, ahead, 1).reshape(tiles, TILE, width)
            turned = pltpu.roll(moved, skew, 1)
            late = jnp.where(sub < skew, turned, 0.0)
            soon = turned - late
            blank = jnp.zeros((1, TILE, width), jnp.float32)
            grown = jnp.concatenate([soon, blank], 0) + jnp.concatenate([blank, late], 0)
            grown = grown.reshape(width + TILE, width)
            sums[part, rows, :width] += jnp.where(outside, 0.0, grown)
            sums[part, rows, width:] += jnp.where(outside, grown, 0.0)

        deposit(0, pro_r * chi_r + pro_i * chi_i)
        deposit(1, pro_r * chi_i - pro_i * chi_r)
        deposit(2, weight * live)
        terms = (
            win_r * chi_r + win_i * chi_i,
            win_r * chi_i - win_i * chi_r,
            (win_r * win_r + win_i * win_i) * live,
        )
        total = terms if total is None else tuple(a + b for a, b in zip(total, terms))
    for part in range(3):
        probe_sums[part] = total[part]


def slot_sums(starts, count, field, probe, amps, tables):
    width = probe.shape[1]
    vmem = pl.BlockSpec(memory_space=pltpu.VMEM)
    smem = pl.BlockSpec(memory_space=pltpu.SMEM)
    slots = amps.shape[0]
    return pl.pallas_call(
        slots_kernel,
        out_shape=(
            jax.ShapeDtypeStruct((3,) + field.shape[1:], jnp.float32),
            jax.ShapeDtypeStruct((3, width, width), jnp.float32),
        ),
        in_specs=[smem, smem, vmem, vmem, vmem, vmem],
        out_specs=(vmem, vmem),
        compiler_params=pltpu.CompilerParams(vmem_limit_bytes=24 * 1024 * 1024),
        cost_estimate=pl.CostEstimate(
            flops=slots * 4 * 2 * 3 * width * width * width * 4,
            bytes_accessed=4 * 1024 * 1024,
            transcendentals=slots * width * width,
        ),
    )(starts, count, field, probe, amps, tables)


def shift(value, axis, step):
    count = lax.axis_size(axis)
    pairs = [(i, i + step) for i in range(count) if 0 <= i + step < count]
    return lax.ppermute(value, axis, pairs)


def swap(value, axis, bit):
    return lax.ppermute(value, axis, [(i, i ^ bit) for i in range(lax.axis_size(axis))])


def together(*values):
    return lax.optimization_barrier(values)


def extend(tile):
    side = tile.shape[2]
    above = shift(tile[:, side - RIM :], "row", 1)
    below = shift(tile[:, :RIM], "row", -1)
    tall = jnp.concatenate([above, tile, below, jnp.zeros_like(tile[:, :TILE])], 1)
    before = shift(jnp.concatenate([tall[0, :, side - RIM :], tall[1, :, side - RIM :]], 1), "col", 1)
    after = shift(jnp.concatenate([tall[0, :, :RIM], tall[1, :, :RIM]], 1), "col", -1)
    sides = jnp.stack(
        [
            jnp.concatenate([after[:, :RIM], before[:, :RIM]], 1),
            jnp.concatenate([after[:, RIM:], before[:, RIM:]], 1),
        ]
    )
    return jnp.concatenate([tall, sides], 2)


def fold(sums, side):
    before = shift(sums[:, :, side : side + RIM], "col", 1)
    after = shift(sums[:, :, side + RIM :], "col", -1)
    tall = sums[:, :, :side] + jnp.concatenate([before, after], 2)
    above = shift(tall[:, RIM + side : 2 * RIM + side], "row", 1)
    below = shift(tall[:, :RIM], "row", -1)
    return tall[:, RIM : RIM + side] + jnp.concatenate([above, below], 1)


def total_over_devices(value):
    rows = value.shape[0] * value.shape[1]
    flat = value.reshape(rows, value.shape[2])
    half = rows // 2
    odd = lax.axis_index("col") % 2
    keep = jnp.where(odd == 0, flat[:half], flat[half:])
    give = jnp.where(odd == 0, flat[half:], flat[:half])
    part = keep + swap(give, "col", 1)
    for axis, first in (("col", 2), ("row", 1)):
        bit = first
        while bit < lax.axis_size(axis):
            part = part + swap(part, axis, bit)
            bit *= 2
    other = swap(part, "col", 1)
    low = jnp.where(odd == 0, part, other)
    high = jnp.where(odd == 0, other, part)
    return jnp.concatenate([low, high], 0).reshape(value.shape)


def body(object_field, probe, positions, counts, amplitude):
    side = object_field.shape[1]
    width = probe.shape[1]
    tables = jnp.asarray(dft_tables(width))
    tile = object_field
    current = probe
    for step in range(positions.shape[2]):
        field = extend(tile)
        starts = positions[0, 0, step].reshape(-1)
        count = counts[0, 0, step].reshape(1)
        sums, probe_sums = slot_sums(starts, count, field, current, amplitude[0, 0, step], tables)
        totals = total_over_devices(probe_sums)
        folded = fold(sums, side)
        tile = tile + folded[0:2] / (folded[2] + 0.1)[None]
        current = current + totals[0:2] / (totals[2] + 0.1)[None]
    return (tile, current)


def solution(mesh):
    return jax.shard_map(
        body,
        mesh=mesh,
        in_specs=(
            P(None, "row", "col"),
            P(),
            P("row", "col", None, None, None),
            P("row", "col", None),
            P("row", "col", None, None, None, None),
        ),
        out_specs=(P(None, "row", "col"), P()),
        check_vma=False,
    )
```

```python
import math

import jax
import jax.numpy as jnp
import numpy as np
from jax import lax
from jax.experimental import pallas as pl
from jax.experimental.pallas import tpu as pltpu
from jax.sharding import PartitionSpec as P

RIM = 64
TILE = 8
EPS = 0.1
MIB = 1024 * 1024


def dft_tables(size):
    index = np.arange(size)
    angle = (index[:, None] * index[None, :] % size) * (-2.0 * math.pi / size)
    cosine = np.cos(angle) / math.sqrt(size)
    sine = np.sin(angle) / math.sqrt(size)
    full = np.block([[cosine, -sine], [sine, cosine]]).astype(np.float32)
    flip = np.ascontiguousarray(full.T)
    tables = []
    for table in (full, flip):
        high = table.astype(jnp.bfloat16)
        tables += [high, (table - high.astype(np.float32)).astype(jnp.bfloat16)]
    return np.stack(tables)


def split(value):
    high = value.astype(jnp.bfloat16)
    return high, (value - high.astype(jnp.float32)).astype(jnp.bfloat16)


def mul(left, right):
    return jnp.dot(left, right, preferred_element_type=jnp.float32)


def left_product(high, low, value):
    first, second = split(value)
    return mul(high, first) + (mul(high, second) + mul(low, first))


def right_product(value, high, low):
    first, second = split(value)
    return mul(first, high) + (mul(second, high) + mul(first, low))


def lanes(shape):
    return lax.broadcasted_iota(jnp.int32, shape, 1)


def pack(real, imag):
    half = real.shape[1] // 2
    first = lanes(real.shape) < half
    low = jnp.where(first, real, pltpu.roll(imag, half, 1))
    high = jnp.where(first, pltpu.roll(real, half, 1), imag)
    return low, high


def unpack(low, high):
    half = low.shape[1] // 2
    first = lanes(low.shape) < half
    real = jnp.where(first, low, pltpu.roll(high, half, 1))
    imag = jnp.where(first, pltpu.roll(low, half, 1), high)
    return real, imag


def grow_rows(term, skew):
    count, width = term.shape
    tiles = count // TILE
    sub = lax.broadcasted_iota(jnp.int32, (tiles, TILE, width), 1)
    turned = pltpu.roll(term.reshape(tiles, TILE, width), skew, 1)
    late = jnp.where(sub < skew, turned, 0.0)
    soon = jnp.where(sub < skew, 0.0, turned)
    blank = jnp.zeros((1, TILE, width), jnp.float32)
    grown = jnp.concatenate([soon, blank], 0) + jnp.concatenate([blank, late], 0)
    return grown.reshape(count + TILE, width)


def lane_turn(col, width):
    return jnp.where(col < 0, col + width, col)


def strips_kernel(place, tile, meta, above, below, tall, near, far):
    side = tile.shape[1]
    odd = place[0] != 0
    for part in range(2):
        tall[part, :RIM] = above[part * RIM : (part + 1) * RIM]
        tall[part, RIM : RIM + side] = tile[part]
        tall[part, RIM + side :] = below[part * RIM : (part + 1) * RIM]
    low, high = pack(tall[0], tall[1])
    rows = low.shape[0]
    near[:rows] = jnp.where(odd, low, high)
    far[:rows] = jnp.where(odd, high, low)
    for out in (near, far):
        out[rows : rows + TILE] = above[2 * RIM :]
        out[rows + TILE : rows + 2 * TILE] = meta[...]
        out[rows + 2 * TILE :] = below[2 * RIM :]


def slots_kernel(
    place, starts, count, tall, near, far, probe, amps, tables,
    core_out, far_out, keep_out, tall_out, field, sums, totals,
):
    width = probe.shape[1]
    rows_all = tall.shape[1]
    tiles = width // TILE
    odd = place[0] != 0
    lane = lanes((width + TILE, width))
    sub = lax.broadcasted_iota(jnp.int32, (tiles, TILE, width), 1)
    from_near, from_far = near[:rows_all], far[:rows_all]
    sides = unpack(jnp.where(odd, from_far, from_near), jnp.where(odd, from_near, from_far))
    for part in range(2):
        field[part, :rows_all, :width] = tall[part]
        field[part, :rows_all, width:] = sides[part]
        field[part, rows_all:] = jnp.zeros_like(field[part, rows_all:])
    sums[...] = jnp.zeros_like(sums)
    full_h, full_l, flip_h, flip_l = (tables[k] for k in range(4))
    pro_r, pro_i = probe[0], probe[1]
    total = None
    for slot in range(amps.shape[0]):
        row = starts[2 * slot] + RIM
        col = starts[2 * slot + 1]
        live = jnp.where(slot < count[0], 1.0, 0.0).astype(jnp.float32)
        base = pl.multiple_of(row // TILE * TILE, TILE)
        rows = pl.ds(base, width + TILE)
        skew = row - base
        lift = jnp.where(skew > 0, TILE - skew, 0)
        ahead = lane_turn(col, width)
        back = lane_turn(-col, width)
        outside = (lane < col) | (lane >= width + col)

        def window(part):
            mixed = jnp.where(outside, field[part, rows, width:], field[part, rows, :width])
            turned = pltpu.roll(mixed.reshape(tiles + 1, TILE, width), lift, 1)
            lined = jnp.where(sub < TILE - skew, turned[:-1], turned[1:])
            return pltpu.roll(lined.reshape(width, width), back, 1)

        win_r, win_i = window(0), window(1)
        psi_r = pro_r * win_r - pro_i * win_i
        psi_i = pro_r * win_i + pro_i * win_r
        half = left_product(full_h, full_l, jnp.concatenate([psi_r, psi_i], 0))
        wave = right_product(jnp.concatenate([half[:width], half[width:]], 1), flip_h, flip_l)
        far_r, far_i = wave[:, :width], wave[:, width:]
        factor = amps[slot] * lax.rsqrt(jnp.maximum(far_r * far_r + far_i * far_i, 1.0))
        half = left_product(
            flip_h, flip_l, jnp.concatenate([far_r * factor, far_i * factor], 0)
        )
        wave = right_product(jnp.concatenate([half[:width], half[width:]], 1), full_h, full_l)
        chi_r = (wave[:, :width] - psi_r) * live
        chi_i = (wave[:, width:] - psi_i) * live

        def deposit(part, term):
            grown = grow_rows(pltpu.roll(term, ahead, 1), skew)
            sums[part, rows, :width] += jnp.where(outside, 0.0, grown)
            sums[part, rows, width:] += jnp.where(outside, grown, 0.0)

        deposit(0, pro_r * chi_r + pro_i * chi_i)
        deposit(1, pro_r * chi_i - pro_i * chi_r)
        terms = (
            win_r * chi_r + win_i * chi_i,
            win_r * chi_i - win_i * chi_r,
            (win_r * win_r + win_i * win_i) * live,
        )
        total = terms if total is None else tuple(a + b for a, b in zip(total, terms))
    half = width // 2
    for part in range(3):
        totals[part] = total[part]
    kept = pl.ds(pl.multiple_of(place[0] * half, half), half)
    given = pl.ds(pl.multiple_of((1 - place[0]) * half, half), half)
    for part in range(3):
        keep_out[part * half : (part + 1) * half] = totals[part, kept]
        core_out[part * half : (part + 1) * half] = totals[part, given]
    for part in range(2):
        tall_out[part] = sums[part, :rows_all, :width]
    low, high = pack(sums[0, :rows_all, width:], sums[1, :rows_all, width:])
    core_out[3 * half :] = jnp.where(odd, high, low)
    far_out[...] = jnp.where(odd, low, high)


def fold_kernel(place, tall, near, far, up, down):
    rows = up.shape[1]
    start = near.shape[0] - tall.shape[1]
    odd = place[0] != 0
    from_near, from_far = near[start:], far[...]
    extra = unpack(jnp.where(odd, from_near, from_far), jnp.where(odd, from_far, from_near))
    for part in range(2):
        whole = tall[part] + extra[part]
        up[part] = whole[:rows]
        down[part] = whole[rows:]


def weight_kernel(metas, probe, out, spread, *, step, slots):
    width = probe.shape[1]
    stride = metas.shape[1]
    lane = lanes((width + TILE, width))
    spread[...] = jnp.zeros_like(spread)
    weight = probe[0] * probe[0] + probe[1] * probe[1]
    for index in range(metas.shape[0]):
        count = metas[index, step * (2 * slots + 1) + 2 * slots]
        for slot in range(slots):
            where = step * (2 * slots + 1) + 2 * slot
            row = metas[index, where] + (RIM + width + (index // 3 - 1) * width)
            col = metas[index, where + 1] + (index % 3 - 1) * width

            @pl.when((slot < count) & (col < width) & (col > -width))
            def _():
                base = pl.multiple_of(row // TILE * TILE, TILE)
                turned = pltpu.roll(weight, lane_turn(col, width), 1)
                grown = grow_rows(turned, row - base)
                inside = (lane >= col) & (lane < width + col)
                spread[pl.ds(base, width + TILE)] += jnp.where(inside, grown, 0.0)

    out[...] = spread[width : width + out.shape[0]]


def update_kernel(place, tall, up, down, above, below, weight, new_tall, near, far):
    rows = up.shape[1]
    odd = place[0] != 0
    first = jnp.where(place[1] != 0, 1.0, 0.0).astype(jnp.float32)
    last = jnp.where(place[2] != 0, 1.0, 0.0).astype(jnp.float32)
    for part in range(2):
        head = tall[part, :rows] + (up[part] + above[part]) / (weight[:rows] + EPS)
        tail = tall[part, rows:] + (down[part] + below[part]) / (weight[rows:] + EPS)
        new_tall[part, :RIM] = head[:RIM] * first
        new_tall[part, RIM:rows] = head[RIM:]
        new_tall[part, rows : 2 * rows - RIM] = tail[: rows - RIM]
        new_tall[part, 2 * rows - RIM :] = tail[rows - RIM :] * last
    low, high = pack(new_tall[0], new_tall[1])
    near[...] = jnp.where(odd, low, high)
    far[...] = jnp.where(odd, high, low)


def call(kernel, shapes, smem_count, operands, flops=1000000, moved=MIB, scratch=(), limit=16):
    vmem = pl.BlockSpec(memory_space=pltpu.VMEM)
    smem = pl.BlockSpec(memory_space=pltpu.SMEM)
    return pl.pallas_call(
        kernel,
        out_shape=tuple(jax.ShapeDtypeStruct(shape, jnp.float32) for shape in shapes),
        in_specs=[smem] * smem_count + [vmem] * (len(operands) - smem_count),
        out_specs=tuple(vmem for _ in shapes),
        scratch_shapes=[pltpu.VMEM(shape, jnp.float32) for shape in scratch],
        compiler_params=pltpu.CompilerParams(vmem_limit_bytes=limit * MIB),
        cost_estimate=pl.CostEstimate(flops=flops, bytes_accessed=moved, transcendentals=0),
    )(*operands)


def shift(value, axis, step):
    count = lax.axis_size(axis)
    pairs = [(i, i + step) for i in range(count) if 0 <= i + step < count]
    return lax.ppermute(value, axis, pairs)


def swap(value, axis, bit):
    return lax.ppermute(value, axis, [(i, i ^ bit) for i in range(lax.axis_size(axis))])


def swap_far(value):
    count = lax.axis_size("col")
    pairs = [(i, i + 1) for i in range(1, count - 1, 2)]
    return lax.ppermute(value, "col", pairs + [(j, i) for i, j in pairs])


def sum_over_chips(part):
    bits = [("row", 1)]
    bit = 2
    while bit < lax.axis_size("col"):
        bits.append(("col", bit))
        bit *= 2
    bit = 2
    while bit < lax.axis_size("row"):
        bits.append(("row", bit))
        bit *= 2
    for axis, bit in bits:
        part = part + swap(part, axis, bit)
    return part


def body(object_field, probe, positions, counts, amplitude):
    side = object_field.shape[1]
    width = probe.shape[1]
    half = width // 2
    steps = positions.shape[2]
    slots = positions.shape[3]
    tall_rows = side + 2 * RIM
    odd = lax.axis_index("col") % 2
    row = lax.axis_index("row")
    place = jnp.stack([odd, row, lax.axis_size("row") - 1 - row]).astype(jnp.int32)
    tables = jnp.asarray(dft_tables(width))

    own = jnp.concatenate([positions[0, 0].reshape(steps, 2 * slots), counts[0, 0][:, None]], 1)
    own = own.reshape(1, -1).astype(jnp.float32)
    meta = jnp.pad(own, ((0, TILE - 1), (0, width - own.shape[1])))
    flat = 2 * RIM
    above = shift(
        jnp.concatenate([object_field[:, side - RIM :].reshape(flat, width), meta], 0), "row", 1
    )
    below = shift(jnp.concatenate([object_field[:, :RIM].reshape(flat, width), meta], 0), "row", -1)
    strip = (tall_rows + 3 * TILE, width)
    tall, near, far = call(
        strips_kernel,
        ((2, tall_rows, side), strip, strip),
        1,
        (place, object_field, meta, above, below),
    )
    near, far = swap(near, "col", 1), swap_far(far)

    def three(value):
        return value[tall_rows:].reshape(3, TILE, width)[:, 0, : own.shape[1]]

    here = jnp.stack([above[flat], meta[0], below[flat]])[:, : own.shape[1]]
    left = jnp.where(odd != 0, three(near), three(far))
    right = jnp.where(odd != 0, three(far), three(near))
    metas = jnp.stack([left, here, right], 1).reshape(9, own.shape[1]).astype(jnp.int32)

    current = probe
    for step in range(steps):
        starts = positions[0, 0, step].reshape(-1)
        count = counts[0, 0, step].reshape(1)
        core, out_far, kept, sums = call(
            slots_kernel,
            (
                (3 * half + tall_rows, width),
                (tall_rows, width),
                (3 * half, width),
                (2, tall_rows, width),
            ),
            3,
            (place, starts, count, tall, near, far, current, amplitude[0, 0, step], tables),
            flops=slots * 96 * width * width * width,
            moved=4 * MIB,
            scratch=(
                (2, tall_rows + TILE, 2 * width),
                (2, tall_rows + TILE, 2 * width),
                (3, width, width),
            ),
            limit=24,
        )
        core = swap(core, "col", 1)
        out_far = swap_far(out_far)
        part = sum_over_chips(kept + core[: 3 * half])
        up, down = call(
            fold_kernel,
            ((2, tall_rows // 2, width), (2, tall_rows // 2, width)),
            1,
            (place, sums, core, out_far),
        )
        (weight,) = call(
            lambda *refs, step=step: weight_kernel(*refs, step=step, slots=slots),
            ((tall_rows, width),),
            1,
            (metas, current),
            scratch=((tall_rows + 2 * width + TILE, width),),
        )
        mine = lax.dynamic_slice_in_dim(current, odd * half, half, 1)
        part = part.reshape(3, half, width)
        mine = mine + part[:2] / (part[2] + EPS)[None]
        if step < steps - 1:
            above = shift(down, "row", 1)
            below = shift(up, "row", -1)
            tall, near, far = call(
                update_kernel,
                ((2, tall_rows, side), (tall_rows, width), (tall_rows, width)),
                1,
                (place, tall, up, down, above, below, weight),
            )
            far = swap_far(far)
            other = swap(jnp.concatenate([near, mine.reshape(2 * half, width)], 0), "col", 1)
            near = other
            other = other[tall_rows:].reshape(2, half, width)
        else:
            above = shift(down[:, side - RIM :], "row", 1)
            below = shift(up[:, :RIM], "row", -1)
            num = jnp.concatenate([up[:, RIM:] + above, down[:, : side - RIM] + below], 1)
            tile = tall[:, RIM : RIM + side] + num / (weight[RIM : RIM + side] + EPS)[None]
            other = swap(mine, "col", 1)
        low = jnp.where(odd == 0, mine, other)
        high = jnp.where(odd == 0, other, mine)
        current = jnp.concatenate([low, high], 1)
    return (tile, current)


def solution(mesh):
    return jax.shard_map(
        body,
        mesh=mesh,
        in_specs=(
            P(None, "row", "col"),
            P(),
            P("row", "col", None, None, None),
            P("row", "col", None),
            P("row", "col", None, None, None, None),
        ),
        out_specs=(P(None, "row", "col"), P()),
        check_vma=False,
    )
```

```python
import math

import jax
import jax.numpy as jnp
import numpy as np
from jax import lax
from jax.experimental import pallas as pl
from jax.experimental.pallas import tpu as pltpu
from jax.sharding import PartitionSpec as P

RIM = 64
TILE = 8
EPS = 0.1
AXES = ("row", "col")
MIB = 1024 * 1024


def dft_tables(size):
    index = np.arange(size)
    angle = (index[:, None] * index[None, :] % size) * (-2.0 * math.pi / size)
    cosine = np.cos(angle) / math.sqrt(size)
    sine = np.sin(angle) / math.sqrt(size)
    full = np.block([[cosine, -sine], [sine, cosine]]).astype(np.float32)
    flip = np.ascontiguousarray(full.T)
    tables = []
    for table in (full, flip):
        high = table.astype(jnp.bfloat16)
        tables += [high, (table - high.astype(np.float32)).astype(jnp.bfloat16)]
    return np.stack(tables)


def split(value):
    high = value.astype(jnp.bfloat16)
    return high, (value - high.astype(jnp.float32)).astype(jnp.bfloat16)


def mul(left, right):
    return jnp.dot(left, right, preferred_element_type=jnp.float32)


def left_product(high, low, value):
    first, second = split(value)
    return mul(high, first) + (mul(high, second) + mul(low, first))


def right_product(value, high, low):
    first, second = split(value)
    return mul(first, high) + (mul(second, high) + mul(first, low))


def lanes(shape):
    return lax.broadcasted_iota(jnp.int32, shape, 1)


def pack(real, imag):
    half = real.shape[1] // 2
    first = lanes(real.shape) < half
    low = jnp.where(first, real, pltpu.roll(imag, half, 1))
    high = jnp.where(first, pltpu.roll(real, half, 1), imag)
    return low, high


def unpack(low, high):
    half = low.shape[1] // 2
    first = lanes(low.shape) < half
    real = jnp.where(first, low, pltpu.roll(high, half, 1))
    imag = jnp.where(first, pltpu.roll(low, half, 1), high)
    return real, imag


def grow_rows(term, skew):
    count, width = term.shape
    tiles = count // TILE
    sub = lax.broadcasted_iota(jnp.int32, (tiles, TILE, width), 1)
    turned = pltpu.roll(term.reshape(tiles, TILE, width), skew, 1)
    late = jnp.where(sub < skew, turned, 0.0)
    soon = jnp.where(sub < skew, 0.0, turned)
    blank = jnp.zeros((1, TILE, width), jnp.float32)
    grown = jnp.concatenate([soon, blank], 0) + jnp.concatenate([blank, late], 0)
    return grown.reshape(count + TILE, width)


def lane_turn(col, width):
    return jnp.where(col < 0, col + width, col)


def strips_kernel(place, tile, meta, first, second, tall, near, far):
    side = tile.shape[1]
    odd, odd_row = place[0] != 0, place[1] != 0
    above = jnp.where(place[2] != 0, jnp.where(odd_row, first[...], second[...]), 0.0)
    below = jnp.where(place[3] != 0, jnp.where(odd_row, second[...], first[...]), 0.0)
    for part in range(2):
        tall[part, :RIM] = above[part * RIM : (part + 1) * RIM]
        tall[part, RIM : RIM + side] = tile[part]
        tall[part, RIM + side :] = below[part * RIM : (part + 1) * RIM]
    low, high = pack(tall[0], tall[1])
    rows = low.shape[0]
    near[:rows] = jnp.where(odd, low, high)
    far[:rows] = jnp.where(odd, high, low)
    for out in (near, far):
        out[rows : rows + TILE] = above[2 * RIM :]
        out[rows + TILE : rows + 2 * TILE] = meta[...]
        out[rows + 2 * TILE :] = below[2 * RIM :]


def slots_kernel(
    place, starts, count, tall, near, far, probe, amps, tables,
    core_out, far_out, keep_out, tall_out, field, sums, totals,
):
    width = probe.shape[1]
    rows_all = tall.shape[1]
    tiles = width // TILE
    odd = place[0] != 0
    lane = lanes((width + TILE, width))
    sub = lax.broadcasted_iota(jnp.int32, (tiles, TILE, width), 1)
    from_near, from_far = near[:rows_all], jnp.where(place[4] != 0, far[:rows_all], 0.0)
    sides = unpack(jnp.where(odd, from_far, from_near), jnp.where(odd, from_near, from_far))
    for part in range(2):
        field[part, :rows_all, :width] = tall[part]
        field[part, :rows_all, width:] = sides[part]
        field[part, rows_all:] = jnp.zeros_like(field[part, rows_all:])
    sums[...] = jnp.zeros_like(sums)
    full_h, full_l, flip_h, flip_l = (tables[k] for k in range(4))
    pro_r, pro_i = probe[0], probe[1]
    total = None
    for slot in range(amps.shape[0]):
        row = starts[2 * slot] + RIM
        col = starts[2 * slot + 1]
        live = jnp.where(slot < count[0], 1.0, 0.0).astype(jnp.float32)
        base = pl.multiple_of(row // TILE * TILE, TILE)
        rows = pl.ds(base, width + TILE)
        skew = row - base
        lift = jnp.where(skew > 0, TILE - skew, 0)
        ahead = lane_turn(col, width)
        back = lane_turn(-col, width)
        outside = (lane < col) | (lane >= width + col)

        def window(part):
            mixed = jnp.where(outside, field[part, rows, width:], field[part, rows, :width])
            turned = pltpu.roll(mixed.reshape(tiles + 1, TILE, width), lift, 1)
            lined = jnp.where(sub < TILE - skew, turned[:-1], turned[1:])
            return pltpu.roll(lined.reshape(width, width), back, 1)

        win_r, win_i = window(0), window(1)
        psi_r = pro_r * win_r - pro_i * win_i
        psi_i = pro_r * win_i + pro_i * win_r
        half = left_product(full_h, full_l, jnp.concatenate([psi_r, psi_i], 0))
        wave = right_product(jnp.concatenate([half[:width], half[width:]], 1), flip_h, flip_l)
        far_r, far_i = wave[:, :width], wave[:, width:]
        factor = amps[slot] * lax.rsqrt(jnp.maximum(far_r * far_r + far_i * far_i, 1.0))
        half = left_product(
            flip_h, flip_l, jnp.concatenate([far_r * factor, far_i * factor], 0)
        )
        wave = right_product(jnp.concatenate([half[:width], half[width:]], 1), full_h, full_l)
        chi_r = (wave[:, :width] - psi_r) * live
        chi_i = (wave[:, width:] - psi_i) * live

        def deposit(part, term):
            grown = grow_rows(pltpu.roll(term, ahead, 1), skew)
            sums[part, rows, :width] += jnp.where(outside, 0.0, grown)
            sums[part, rows, width:] += jnp.where(outside, grown, 0.0)

        deposit(0, pro_r * chi_r + pro_i * chi_i)
        deposit(1, pro_r * chi_i - pro_i * chi_r)
        terms = (
            win_r * chi_r + win_i * chi_i,
            win_r * chi_i - win_i * chi_r,
            (win_r * win_r + win_i * win_i) * live,
        )
        total = terms if total is None else tuple(a + b for a, b in zip(total, terms))
    half = width // 2
    for part in range(3):
        totals[part] = total[part]
    kept = pl.ds(pl.multiple_of(place[0] * half, half), half)
    given = pl.ds(pl.multiple_of((1 - place[0]) * half, half), half)
    for part in range(3):
        keep_out[part * half : (part + 1) * half] = totals[part, kept]
        core_out[part * half : (part + 1) * half] = totals[part, given]
    for part in range(2):
        tall_out[part] = sums[part, :rows_all, :width]
    low, high = pack(sums[0, :rows_all, width:], sums[1, :rows_all, width:])
    core_out[3 * half :] = jnp.where(odd, high, low)
    far_out[...] = jnp.where(odd, low, high)


def folded(place, tall, near, far):
    start = near.shape[0] - tall.shape[1]
    odd = place[0] != 0
    from_near, from_far = near[start:], jnp.where(place[4] != 0, far[...], 0.0)
    extra = unpack(jnp.where(odd, from_near, from_far), jnp.where(odd, from_far, from_near))
    return tall[0] + extra[0], tall[1] + extra[1]


def fold_kernel(place, tall, near, far, first, second):
    rows = first.shape[1]
    odd_row = place[1] != 0
    whole = folded(place, tall, near, far)
    for part in range(2):
        up, down = whole[part][:rows], whole[part][rows:]
        first[part] = jnp.where(odd_row, up, down)
        second[part] = jnp.where(odd_row, down, up)


def last_fold_kernel(place, tall, near, far, middle, first, second):
    rows = middle.shape[1]
    odd_row = place[1] != 0
    whole = folded(place, tall, near, far)
    for part in range(2):
        up, down = whole[part][:RIM], whole[part][RIM + rows :]
        middle[part] = whole[part][RIM : RIM + rows]
        first[part] = jnp.where(odd_row, up, down)
        second[part] = jnp.where(odd_row, down, up)


def weight_kernel(metas, probe, out, spread, *, step, slots):
    width = probe.shape[1]
    stride = metas.shape[1]
    lane = lanes((width + TILE, width))
    spread[...] = jnp.zeros_like(spread)
    weight = probe[0] * probe[0] + probe[1] * probe[1]
    for index in range(metas.shape[0]):
        count = metas[index, step * (2 * slots + 1) + 2 * slots]
        for slot in range(slots):
            where = step * (2 * slots + 1) + 2 * slot
            row = metas[index, where] + (RIM + width + (index // 3 - 1) * width)
            col = metas[index, where + 1] + (index % 3 - 1) * width

            @pl.when((slot < count) & (col < width) & (col > -width))
            def _():
                base = pl.multiple_of(row // TILE * TILE, TILE)
                turned = pltpu.roll(weight, lane_turn(col, width), 1)
                grown = grow_rows(turned, row - base)
                inside = (lane >= col) & (lane < width + col)
                spread[pl.ds(base, width + TILE)] += jnp.where(inside, grown, 0.0)

    out[...] = spread[width : width + out.shape[0]]


def update_kernel(place, tall, sent_1, sent_2, got_1, got_2, weight, new_tall, near, far):
    rows = sent_1.shape[1]
    odd, odd_row = place[0] != 0, place[1] != 0
    for part in range(2):
        up = jnp.where(odd_row, sent_1[part], sent_2[part])
        down = jnp.where(odd_row, sent_2[part], sent_1[part])
        above = jnp.where(odd_row, got_1[part], got_2[part])
        below = jnp.where(odd_row, got_2[part], got_1[part])
        up = up + jnp.where(place[2] != 0, above, 0.0)
        down = down + jnp.where(place[3] != 0, below, 0.0)
        head = tall[part, :rows] + up / (weight[:rows] + EPS)
        tail = tall[part, rows:] + down / (weight[rows:] + EPS)
        new_tall[part, :RIM] = jnp.where(place[2] != 0, head[:RIM], 0.0)
        new_tall[part, RIM:rows] = head[RIM:]
        new_tall[part, rows : 2 * rows - RIM] = tail[: rows - RIM]
        new_tall[part, 2 * rows - RIM :] = jnp.where(place[3] != 0, tail[rows - RIM :], 0.0)
    low, high = pack(new_tall[0], new_tall[1])
    near[...] = jnp.where(odd, low, high)
    far[...] = jnp.where(odd, high, low)


def last_kernel(place, tall, middle, got_1, got_2, weight, tile):
    side = tile.shape[1]
    odd_row = place[1] != 0
    for part in range(2):
        above = jnp.where(odd_row, got_1[part], got_2[part])
        below = jnp.where(odd_row, got_2[part], got_1[part])
        above = jnp.where(place[2] != 0, above, 0.0)
        below = jnp.where(place[3] != 0, below, 0.0)
        num = middle[part] + jnp.concatenate([above, below], 0)
        tile[part] = tall[part, RIM : RIM + side] + num / (weight[RIM : RIM + side] + EPS)


def call(kernel, shapes, smem_count, operands, flops=1000000, moved=MIB, scratch=(), limit=16):
    vmem = pl.BlockSpec(memory_space=pltpu.VMEM)
    smem = pl.BlockSpec(memory_space=pltpu.SMEM)
    return pl.pallas_call(
        kernel,
        out_shape=tuple(jax.ShapeDtypeStruct(shape, jnp.float32) for shape in shapes),
        in_specs=[smem] * smem_count + [vmem] * (len(operands) - smem_count),
        out_specs=tuple(vmem for _ in shapes),
        scratch_shapes=[pltpu.VMEM(shape, jnp.float32) for shape in scratch],
        compiler_params=pltpu.CompilerParams(vmem_limit_bytes=limit * MIB),
        cost_estimate=pl.CostEstimate(flops=flops, bytes_accessed=moved, transcendentals=0),
    )(*operands)


def swap(value, axis, bit):
    return lax.ppermute(value, axis, [(i, i ^ bit) for i in range(lax.axis_size(axis))])


def swap_far(value):
    rows, cols = lax.axis_size("row"), lax.axis_size("col")
    pairs = []
    for row in range(rows):
        for col in range(cols):
            to_row, to_col = row, col + (1 if col % 2 else -1)
            if not 0 <= to_col < cols:
                to_row, to_col = row ^ 1, col
            pairs.append((row * cols + col, to_row * cols + to_col))
    return lax.ppermute(value, AXES, pairs)


def swap_rows(value):
    rows, cols = lax.axis_size("row"), lax.axis_size("col")
    pairs = []
    for row in range(rows):
        for col in range(cols):
            to_row, to_col = row + (1 if row % 2 else -1), col
            if not 0 <= to_row < rows:
                to_row, to_col = row, col ^ 1
            pairs.append((row * cols + col, to_row * cols + to_col))
    return lax.ppermute(value, AXES, pairs)


def sum_over_chips(part):
    bits = [("row", 1)]
    bit = 2
    while bit < lax.axis_size("col"):
        bits.append(("col", bit))
        bit *= 2
    bit = 2
    while bit < lax.axis_size("row"):
        bits.append(("row", bit))
        bit *= 2
    for axis, bit in bits:
        part = part + swap(part, axis, bit)
    return part


def body(object_field, probe, positions, counts, amplitude):
    side = object_field.shape[1]
    width = probe.shape[1]
    half = width // 2
    steps = positions.shape[2]
    slots = positions.shape[3]
    tall_rows = side + 2 * RIM
    row, col = lax.axis_index("row"), lax.axis_index("col")
    odd, odd_row = col % 2, row % 2
    outer = (col == 0) | (col == lax.axis_size("col") - 1)
    place = jnp.stack([odd, odd_row, row, lax.axis_size("row") - 1 - row, 1 - outer]).astype(jnp.int32)
    tables = jnp.asarray(dft_tables(width))

    own = jnp.concatenate([positions[0, 0].reshape(steps, 2 * slots), counts[0, 0][:, None]], 1)
    own = own.reshape(1, -1).astype(jnp.float32)
    meta = jnp.pad(own, ((0, TILE - 1), (0, width - own.shape[1])))
    flat = 2 * RIM
    up = jnp.concatenate([object_field[:, :RIM].reshape(flat, width), meta], 0)
    down = jnp.concatenate([object_field[:, side - RIM :].reshape(flat, width), meta], 0)
    first = swap(jnp.where(odd_row != 0, up, down), "row", 1)
    second = swap_rows(jnp.where(odd_row != 0, down, up))
    strip = (tall_rows + 3 * TILE, width)
    tall, near, far = call(
        strips_kernel,
        ((2, tall_rows, side), strip, strip),
        1,
        (place, object_field, meta, first, second),
    )
    near, far = swap(near, "col", 1), swap_far(far)

    def three(value):
        return value[tall_rows:].reshape(3, TILE, width)[:, 0, : own.shape[1]]

    above = jnp.where(row > 0, jnp.where(odd_row != 0, first[flat], second[flat]), 0.0)
    below = jnp.where(row < lax.axis_size("row") - 1, jnp.where(odd_row != 0, second[flat], first[flat]), 0.0)
    here = jnp.stack([above, meta[0], below])[:, : own.shape[1]]
    sides = three(near), jnp.where(outer, 0.0, three(far))
    left = jnp.where(odd != 0, sides[0], sides[1])
    right = jnp.where(odd != 0, sides[1], sides[0])
    metas = jnp.stack([left, here, right], 1).reshape(9, own.shape[1]).astype(jnp.int32)

    current = probe
    for step in range(steps):
        starts = positions[0, 0, step].reshape(-1)
        count = counts[0, 0, step].reshape(1)
        core, out_far, kept, sums = call(
            slots_kernel,
            (
                (3 * half + tall_rows, width),
                (tall_rows, width),
                (3 * half, width),
                (2, tall_rows, width),
            ),
            3,
            (place, starts, count, tall, near, far, current, amplitude[0, 0, step], tables),
            flops=slots * 96 * width * width * width,
            moved=4 * MIB,
            scratch=(
                (2, tall_rows + TILE, 2 * width),
                (2, tall_rows + TILE, 2 * width),
                (3, width, width),
            ),
            limit=24,
        )
        core = swap(core, "col", 1)
        out_far = swap_far(out_far)
        part = sum_over_chips(kept + core[: 3 * half])
        (weight,) = call(
            lambda *refs, step=step: weight_kernel(*refs, step=step, slots=slots),
            ((tall_rows, width),),
            1,
            (metas, current),
            scratch=((tall_rows + 2 * width + TILE, width),),
        )
        mine = lax.dynamic_slice_in_dim(current, odd * half, half, 1)
        part = part.reshape(3, half, width)
        mine = mine + part[:2] / (part[2] + EPS)[None]
        if step < steps - 1:
            sent_1, sent_2 = call(
                fold_kernel,
                ((2, tall_rows // 2, width), (2, tall_rows // 2, width)),
                1,
                (place, sums, core, out_far),
            )
            got_1, got_2 = swap(sent_1, "row", 1), swap_rows(sent_2)
            tall, near, far = call(
                update_kernel,
                ((2, tall_rows, side), (tall_rows, width), (tall_rows, width)),
                1,
                (place, tall, sent_1, sent_2, got_1, got_2, weight),
            )
            far = swap_far(far)
            other = swap(jnp.concatenate([near, mine.reshape(2 * half, width)], 0), "col", 1)
            near = other
            other = other[tall_rows:].reshape(2, half, width)
        else:
            middle, sent_1, sent_2 = call(
                last_fold_kernel,
                ((2, side, width), (2, RIM, width), (2, RIM, width)),
                1,
                (place, sums, core, out_far),
            )
            got_1, got_2 = swap(sent_1, "row", 1), swap_rows(sent_2)
            (tile,) = call(
                last_kernel,
                ((2, side, side),),
                1,
                (place, tall, middle, got_1, got_2, weight),
            )
            other = swap(mine, "col", 1)
        low = jnp.where(odd == 0, mine, other)
        high = jnp.where(odd == 0, other, mine)
        current = jnp.concatenate([low, high], 1)
    return (tile, current)


def solution(mesh):
    return jax.shard_map(
        body,
        mesh=mesh,
        in_specs=(
            P(None, "row", "col"),
            P(),
            P("row", "col", None, None, None),
            P("row", "col", None),
            P("row", "col", None, None, None, None),
        ),
        out_specs=(P(None, "row", "col"), P()),
        check_vma=False,
    )
```

```python
import functools
import math

import jax
import jax.numpy as jnp
import numpy as np
from jax import lax
from jax.experimental import pallas as pl
from jax.experimental.pallas import tpu as pltpu
from jax.sharding import PartitionSpec as P

RIM = 64
TILE = 8
EPS = 0.1
AXES = ("row", "col")
MIB = 1024 * 1024


def dft_tables(size):
    index = np.arange(size)
    angle = (index[:, None] * index[None, :] % size) * (-2.0 * math.pi / size)
    cosine = np.cos(angle) / math.sqrt(size)
    sine = np.sin(angle) / math.sqrt(size)
    full = np.block([[cosine, -sine], [sine, cosine]]).astype(np.float32)
    flip = np.ascontiguousarray(full.T)
    tables = []
    for table in (full, flip):
        high = table.astype(jnp.bfloat16)
        tables += [high, (table - high.astype(np.float32)).astype(jnp.bfloat16)]
    return np.stack(tables)


def split(value):
    high = value.astype(jnp.bfloat16)
    return high, (value - high.astype(jnp.float32)).astype(jnp.bfloat16)


def mul(left, right):
    return jnp.dot(left, right, preferred_element_type=jnp.float32)


def left_product(high, low, value):
    first, second = split(value)
    return mul(high, first) + (mul(high, second) + mul(low, first))


def right_product(value, high, low):
    first, second = split(value)
    return mul(first, high) + (mul(second, high) + mul(first, low))


def lanes(shape):
    return lax.broadcasted_iota(jnp.int32, shape, 1)


def pack(real, imag):
    half = real.shape[1] // 2
    first = lanes(real.shape) < half
    low = jnp.where(first, real, pltpu.roll(imag, half, 1))
    high = jnp.where(first, pltpu.roll(real, half, 1), imag)
    return low, high


def unpack(low, high):
    half = low.shape[1] // 2
    first = lanes(low.shape) < half
    real = jnp.where(first, low, pltpu.roll(high, half, 1))
    imag = jnp.where(first, pltpu.roll(low, half, 1), high)
    return real, imag


def grow_rows(term, skew):
    count, width = term.shape
    tiles = count // TILE
    sub = lax.broadcasted_iota(jnp.int32, (tiles, TILE, width), 1)
    turned = pltpu.roll(term.reshape(tiles, TILE, width), skew, 1)
    late = jnp.where(sub < skew, turned, 0.0)
    soon = jnp.where(sub < skew, 0.0, turned)
    blank = jnp.zeros((1, TILE, width), jnp.float32)
    grown = jnp.concatenate([soon, blank], 0) + jnp.concatenate([blank, late], 0)
    return grown.reshape(count + TILE, width)


def lane_turn(col, width):
    return jnp.where(col < 0, col + width, col)


class Spot:
    def __init__(self):
        row, col = lax.axis_index("row"), lax.axis_index("col")
        self.side = lax.rem(col, 2)
        self.odd = self.side != 0
        self.row_side = lax.rem(row, 2)
        self.odd_row = self.row_side != 0
        self.has_above = row != 0
        self.has_below = row != lax.axis_size("row") - 1
        self.has_far = (col != 0) & (col != lax.axis_size("col") - 1)


def first_kernel(tile, scan, first, second, meta, offsets, sems):
    spot = Spot()
    side = tile.shape[1]
    near_edge = pl.multiple_of(spot.row_side * RIM, RIM)
    copies = [pltpu.make_async_copy(scan, offsets, sems.at[0])]
    for part in range(2):
        rows = pl.ds(part * RIM, RIM)
        lower = pl.ds(side - RIM - near_edge, RIM)
        upper = pl.ds(near_edge, RIM)
        copies.append(pltpu.make_async_copy(tile.at[part, lower], first.at[rows], sems.at[1 + part]))
        copies.append(pltpu.make_async_copy(tile.at[part, upper], second.at[rows], sems.at[3 + part]))
    for copy in copies:
        copy.start()
    meta[...] = jnp.zeros_like(meta)
    copies[0].wait()
    meta[: scan.shape[0], : scan.shape[1]] = offsets[...].astype(jnp.float32)
    first[2 * RIM :] = meta[...]
    second[2 * RIM :] = meta[...]
    for copy in copies[1:]:
        copy.wait()


def strips_kernel(tile, meta, first, second, tall, near, far):
    side = tile.shape[1]
    spot = Spot()
    odd, odd_row = spot.odd, spot.odd_row
    above = jnp.where(spot.has_above, jnp.where(odd_row, first[...], second[...]), 0.0)
    below = jnp.where(spot.has_below, jnp.where(odd_row, second[...], first[...]), 0.0)
    for part in range(2):
        tall[part, :RIM] = above[part * RIM : (part + 1) * RIM]
        tall[part, RIM : RIM + side] = tile[part]
        tall[part, RIM + side :] = below[part * RIM : (part + 1) * RIM]
    low, high = pack(tall[0], tall[1])
    rows = low.shape[0]
    near[:rows] = jnp.where(odd, low, high)
    far[:rows] = jnp.where(odd, high, low)
    for out in (near, far):
        out[rows : rows + TILE] = above[2 * RIM :]
        out[rows + TILE : rows + 2 * TILE] = meta[...]
        out[rows + 2 * TILE :] = below[2 * RIM :]


def slots_kernel(
    scan, tall, near, far, probe, amps, tables,
    core_out, far_out, keep_out, tall_out, field, sums, totals, wins, psis, starts, sem, *, step,
):
    fetch = pltpu.make_async_copy(scan, starts, sem)
    fetch.start()
    spot = Spot()
    width = probe.shape[1]
    rows_all = tall.shape[1]
    tiles = width // TILE
    slots = amps.shape[0]
    odd = spot.odd
    lane = lanes((width + TILE, width))
    sub = lax.broadcasted_iota(jnp.int32, (tiles, TILE, width), 1)
    from_near, from_far = near[:rows_all], jnp.where(spot.has_far, far[:rows_all], 0.0)
    sides = unpack(jnp.where(odd, from_far, from_near), jnp.where(odd, from_near, from_far))
    for part in range(2):
        field[part, :rows_all, :width] = tall[part]
        field[part, :rows_all, width:] = sides[part]
        field[part, rows_all:] = jnp.zeros_like(field[part, rows_all:])
    sums[...] = jnp.zeros_like(sums)
    fetch.wait()
    full_h, full_l, flip_h, flip_l = (tables[k] for k in range(4))
    pro_r, pro_i = probe[0], probe[1]

    def where(slot):
        row = starts[3 * step, slot] + RIM
        col = starts[3 * step + 1, slot]
        base = pl.multiple_of(row // TILE * TILE, TILE)
        outside = (lane < col) | (lane >= width + col)
        return pl.ds(base, width + TILE), row - base, col, outside

    total = None
    members = range(slots)
    columns = []
    for slot in members:
        rows, skew, col, outside = where(slot)
        lift = jnp.where(skew > 0, TILE - skew, 0)
        back = lane_turn(-col, width)
        win = []
        for part in range(2):
            mixed = jnp.where(outside, field[part, rows, width:], field[part, rows, :width])
            turned = pltpu.roll(mixed.reshape(tiles + 1, TILE, width), lift, 1)
            lined = jnp.where(sub < TILE - skew, turned[:-1], turned[1:])
            win.append(pltpu.roll(lined.reshape(width, width), back, 1))
            wins[slot, part] = win[part]
        psi_r = pro_r * win[0] - pro_i * win[1]
        psi_i = pro_r * win[1] + pro_i * win[0]
        psis[slot, 0] = psi_r
        psis[slot, 1] = psi_i
        columns.append(jnp.concatenate([psi_r, psi_i], 0))

    def turn(half):
        return jnp.concatenate(
            [
                jnp.concatenate(
                    [half[:width, k * width : (k + 1) * width], half[width:, k * width : (k + 1) * width]], 1
                )
                for k in range(slots)
            ],
            0,
        )

    half = left_product(full_h, full_l, jnp.concatenate(columns, 1))
    wave = right_product(turn(half), flip_h, flip_l)
    columns = []
    for k, slot in enumerate(members):
        far_r, far_i = wave[k * width : (k + 1) * width, :width], wave[k * width : (k + 1) * width, width:]
        factor = amps[slot] * lax.rsqrt(jnp.maximum(far_r * far_r + far_i * far_i, 1.0))
        columns.append(jnp.concatenate([far_r * factor, far_i * factor], 0))
    half = left_product(flip_h, flip_l, jnp.concatenate(columns, 1))
    wave = right_product(turn(half), full_h, full_l)
    for k, slot in enumerate(members):
        rows, skew, col, outside = where(slot)
        ahead = lane_turn(col, width)
        live = jnp.where(slot < starts[3 * step + 2, 0], 1.0, 0.0).astype(jnp.float32)
        win_r, win_i = wins[slot, 0], wins[slot, 1]
        chi_r = (wave[k * width : (k + 1) * width, :width] - psis[slot, 0]) * live
        chi_i = (wave[k * width : (k + 1) * width, width:] - psis[slot, 1]) * live

        def deposit(part, term):
            grown = grow_rows(pltpu.roll(term, ahead, 1), skew)
            sums[part, rows, :width] += jnp.where(outside, 0.0, grown)
            sums[part, rows, width:] += jnp.where(outside, grown, 0.0)

        deposit(0, pro_r * chi_r + pro_i * chi_i)
        deposit(1, pro_r * chi_i - pro_i * chi_r)
        terms = (
            win_r * chi_r + win_i * chi_i,
            win_r * chi_i - win_i * chi_r,
            (win_r * win_r + win_i * win_i) * live,
        )
        total = terms if total is None else tuple(a + b for a, b in zip(total, terms))
    half = width // 2
    for part in range(3):
        totals[part] = total[part]
    kept = pl.ds(pl.multiple_of(spot.side * half, half), half)
    given = pl.ds(pl.multiple_of((1 - spot.side) * half, half), half)
    for part in range(3):
        keep_out[part * half : (part + 1) * half] = totals[part, kept]
        core_out[part * half : (part + 1) * half] = totals[part, given]
    for part in range(2):
        tall_out[part] = sums[part, :rows_all, :width]
    low, high = pack(sums[0, :rows_all, width:], sums[1, :rows_all, width:])
    core_out[3 * half :] = jnp.where(odd, high, low)
    far_out[...] = jnp.where(odd, low, high)


def folded(spot, tall, near, far):
    start = near.shape[0] - tall.shape[1]
    odd = spot.odd
    from_near, from_far = near[start:], jnp.where(spot.has_far, far[...], 0.0)
    extra = unpack(jnp.where(odd, from_near, from_far), jnp.where(odd, from_far, from_near))
    return tall[0] + extra[0], tall[1] + extra[1]


def fold_kernel(tall, near, far, first, second):
    rows = first.shape[1]
    spot = Spot()
    odd_row = spot.odd_row
    whole = folded(spot, tall, near, far)
    for part in range(2):
        up, down = whole[part][:rows], whole[part][rows:]
        first[part] = jnp.where(odd_row, up, down)
        second[part] = jnp.where(odd_row, down, up)


def last_fold_kernel(tall, near, far, middle, first, second):
    rows = middle.shape[1]
    spot = Spot()
    odd_row = spot.odd_row
    whole = folded(spot, tall, near, far)
    for part in range(2):
        up, down = whole[part][:RIM], whole[part][RIM + rows :]
        middle[part] = whole[part][RIM : RIM + rows]
        first[part] = jnp.where(odd_row, up, down)
        second[part] = jnp.where(odd_row, down, up)


def weight_kernel(metas, probe, out, spread, *, step, slots):
    width = probe.shape[1]
    lane = lanes((width + TILE, width))
    spread[...] = jnp.zeros_like(spread)
    weight = probe[0] * probe[0] + probe[1] * probe[1]
    for index in range(metas.shape[0]):
        count = metas[index, (3 * step + 2) * slots]
        for slot in range(slots):
            row = metas[index, 3 * step * slots + slot] + (RIM + width + (index // 3 - 1) * width)
            col = metas[index, (3 * step + 1) * slots + slot] + (index % 3 - 1) * width

            @pl.when((slot < count) & (col < width) & (col > -width))
            def _():
                base = pl.multiple_of(row // TILE * TILE, TILE)
                turned = pltpu.roll(weight, lane_turn(col, width), 1)
                grown = grow_rows(turned, row - base)
                inside = (lane >= col) & (lane < width + col)
                spread[pl.ds(base, width + TILE)] += jnp.where(inside, grown, 0.0)

    out[...] = spread[width : width + out.shape[0]]


def update_kernel(tall, sent_1, sent_2, got_1, got_2, weight, new_tall, near, far):
    rows = sent_1.shape[1]
    spot = Spot()
    odd, odd_row = spot.odd, spot.odd_row
    for part in range(2):
        up = jnp.where(odd_row, sent_1[part], sent_2[part])
        down = jnp.where(odd_row, sent_2[part], sent_1[part])
        above = jnp.where(odd_row, got_1[part], got_2[part])
        below = jnp.where(odd_row, got_2[part], got_1[part])
        up = up + jnp.where(spot.has_above, above, 0.0)
        down = down + jnp.where(spot.has_below, below, 0.0)
        head = tall[part, :rows] + up / (weight[:rows] + EPS)
        tail = tall[part, rows:] + down / (weight[rows:] + EPS)
        new_tall[part, :RIM] = jnp.where(spot.has_above, head[:RIM], 0.0)
        new_tall[part, RIM:rows] = head[RIM:]
        new_tall[part, rows : 2 * rows - RIM] = tail[: rows - RIM]
        new_tall[part, 2 * rows - RIM :] = jnp.where(spot.has_below, tail[rows - RIM :], 0.0)
    low, high = pack(new_tall[0], new_tall[1])
    near[...] = jnp.where(odd, low, high)
    far[...] = jnp.where(odd, high, low)


def last_kernel(tall, middle, got_1, got_2, weight, tile):
    side = tile.shape[1]
    spot = Spot()
    odd_row = spot.odd_row
    for part in range(2):
        above = jnp.where(odd_row, got_1[part], got_2[part])
        below = jnp.where(odd_row, got_2[part], got_1[part])
        above = jnp.where(spot.has_above, above, 0.0)
        below = jnp.where(spot.has_below, below, 0.0)
        num = middle[part] + jnp.concatenate([above, below], 0)
        tile[part] = tall[part, RIM : RIM + side] + num / (weight[RIM : RIM + side] + EPS)


def call(kernel, shapes, places, operands, flops=1000000, moved=MIB, scratch=(), more=(), limit=16):
    vmem = pl.BlockSpec(memory_space=pltpu.VMEM)
    smem = pl.BlockSpec(memory_space=pltpu.SMEM)
    anywhere = pl.BlockSpec(memory_space=pl.ANY)
    return pl.pallas_call(
        kernel,
        out_shape=tuple(jax.ShapeDtypeStruct(shape, jnp.float32) for shape in shapes),
        in_specs=[{"s": smem, "a": anywhere}.get(where, vmem) for where in places.ljust(len(operands), "v")],
        out_specs=tuple(vmem for _ in shapes),
        scratch_shapes=[pltpu.VMEM(shape, jnp.float32) for shape in scratch] + list(more),
        compiler_params=pltpu.CompilerParams(vmem_limit_bytes=limit * MIB),
        cost_estimate=pl.CostEstimate(flops=flops, bytes_accessed=moved, transcendentals=0),
    )(*operands)


def swap(value, axis, bit):
    return lax.ppermute(value, axis, [(i, i ^ bit) for i in range(lax.axis_size(axis))])


def swap_far(value):
    rows, cols = lax.axis_size("row"), lax.axis_size("col")
    pairs = []
    for row in range(rows):
        for col in range(cols):
            to_row, to_col = row, col + (1 if col % 2 else -1)
            if not 0 <= to_col < cols:
                to_row, to_col = row ^ 1, col
            pairs.append((row * cols + col, to_row * cols + to_col))
    return lax.ppermute(value, AXES, pairs)


def swap_rows(value):
    rows, cols = lax.axis_size("row"), lax.axis_size("col")
    pairs = []
    for row in range(rows):
        for col in range(cols):
            to_row, to_col = row + (1 if row % 2 else -1), col
            if not 0 <= to_row < rows:
                to_row, to_col = row, col ^ 1
            pairs.append((row * cols + col, to_row * cols + to_col))
    return lax.ppermute(value, AXES, pairs)


def sum_over_chips(part):
    bits = [("row", 1)]
    bit = 2
    while bit < lax.axis_size("col"):
        bits.append(("col", bit))
        bit *= 2
    bit = 2
    while bit < lax.axis_size("row"):
        bits.append(("row", bit))
        bit *= 2
    for axis, bit in bits:
        part = part + swap(part, axis, bit)
    return part


def body(object_field, probe, positions, counts, amplitude):
    side = object_field.shape[1]
    width = probe.shape[1]
    half = width // 2
    steps = positions.shape[2]
    slots = positions.shape[3]
    tall_rows = side + 2 * RIM
    row, col = lax.axis_index("row"), lax.axis_index("col")
    odd, odd_row = col % 2, row % 2
    outer = (col == 0) | (col == lax.axis_size("col") - 1)
    tables = jnp.asarray(dft_tables(width))

    offsets = jnp.swapaxes(positions[0, 0], 1, 2)
    amount = jnp.broadcast_to(counts[0, 0][:, None, None], (steps, 1, slots))
    scan = jnp.concatenate([offsets, amount], 1).reshape(3 * steps, slots)
    flat = 2 * RIM
    first, second, meta = call(
        first_kernel,
        ((flat + TILE, width), (flat + TILE, width), (TILE, width)),
        "aa",
        (object_field, scan),
        more=(pltpu.VMEM(scan.shape, jnp.int32), pltpu.SemaphoreType.DMA((5,))),
    )
    first, second = swap(first, "row", 1), swap_rows(second)
    strip = (tall_rows + 3 * TILE, width)
    tall, near, far = call(
        strips_kernel,
        ((2, tall_rows, side), strip, strip),
        "",
        (object_field, meta, first, second),
    )
    near, far = swap(near, "col", 1), swap_far(far)

    def three(value):
        return value[tall_rows:].reshape(3, TILE, width)[:, : 3 * steps, :slots]

    above = jnp.where(row > 0, jnp.where(odd_row != 0, first[flat:], second[flat:]), 0.0)
    below = jnp.where(row < lax.axis_size("row") - 1, jnp.where(odd_row != 0, second[flat:], first[flat:]), 0.0)
    here = jnp.stack([above, meta, below])[:, : 3 * steps, :slots]
    sides = three(near), jnp.where(outer, 0.0, three(far))
    left = jnp.where(odd != 0, sides[0], sides[1])
    right = jnp.where(odd != 0, sides[1], sides[0])
    metas = jnp.stack([left, here, right], 1).reshape(9, -1).astype(jnp.int32)

    current = probe
    for step in range(steps):
        core, out_far, kept, sums = call(
            functools.partial(slots_kernel, step=step),
            (
                (3 * half + tall_rows, width),
                (tall_rows, width),
                (3 * half, width),
                (2, tall_rows, width),
            ),
            "a",
            (scan, tall, near, far, current, amplitude[0, 0, step], tables),
            flops=slots * 96 * width * width * width,
            moved=4 * MIB,
            scratch=(
                (2, tall_rows + TILE, 2 * width),
                (2, tall_rows + TILE, 2 * width),
                (3, width, width),
                (slots, 2, width, width),
                (slots, 2, width, width),
            ),
            more=(pltpu.SMEM(scan.shape, jnp.int32), pltpu.SemaphoreType.DMA(())),
            limit=24,
        )
        core = swap(core, "col", 1)
        out_far = swap_far(out_far)
        part = sum_over_chips(kept + core[: 3 * half])
        (weight,) = call(
            functools.partial(weight_kernel, step=step, slots=slots),
            ((tall_rows, width),),
            "s",
            (metas, current),
            scratch=((tall_rows + 2 * width + TILE, width),),
        )
        mine = lax.dynamic_slice_in_dim(current, odd * half, half, 1)
        part = part.reshape(3, half, width)
        mine = mine + part[:2] / (part[2] + EPS)[None]
        if step < steps - 1:
            sent_1, sent_2 = call(
                fold_kernel,
                ((2, tall_rows // 2, width), (2, tall_rows // 2, width)),
                "",
                (sums, core, out_far),
            )
            got_1, got_2 = swap(sent_1, "row", 1), swap_rows(sent_2)
            tall, near, far = call(
                update_kernel,
                ((2, tall_rows, side), (tall_rows, width), (tall_rows, width)),
                "",
                (tall, sent_1, sent_2, got_1, got_2, weight),
            )
            far = swap_far(far)
            other = swap(jnp.concatenate([near, mine.reshape(2 * half, width)], 0), "col", 1)
            near = other
            other = other[tall_rows:].reshape(2, half, width)
        else:
            middle, sent_1, sent_2 = call(
                last_fold_kernel,
                ((2, side, width), (2, RIM, width), (2, RIM, width)),
                "",
                (sums, core, out_far),
            )
            got_1, got_2 = swap(sent_1, "row", 1), swap_rows(sent_2)
            (tile,) = call(
                last_kernel,
                ((2, side, side),),
                "",
                (tall, middle, got_1, got_2, weight),
            )
            other = swap(mine, "col", 1)
        low = jnp.where(odd == 0, mine, other)
        high = jnp.where(odd == 0, other, mine)
        current = jnp.concatenate([low, high], 1)
    return (tile, current)


def solution(mesh):
    return jax.shard_map(
        body,
        mesh=mesh,
        in_specs=(
            P(None, "row", "col"),
            P(),
            P("row", "col", None, None, None),
            P("row", "col", None),
            P("row", "col", None, None, None, None),
        ),
        out_specs=(P(None, "row", "col"), P()),
        check_vma=False,
    )
```

```python
import functools
import math

import jax
import jax.numpy as jnp
import numpy as np
from jax import lax
from jax.experimental import pallas as pl
from jax.experimental.pallas import tpu as pltpu
from jax.sharding import PartitionSpec as P

RIM = 64
TILE = 8
EPS = 0.1
AXES = ("row", "col")
MIB = 1024 * 1024


def dft_tables(size):
    index = np.arange(size)
    angle = (index[:, None] * index[None, :] % size) * (-2.0 * math.pi / size)
    cosine = np.cos(angle) / math.sqrt(size)
    sine = np.sin(angle) / math.sqrt(size)
    full = np.block([[cosine, -sine], [sine, cosine]]).astype(np.float32)
    flip = np.ascontiguousarray(full.T)
    tables = []
    for table in (full, flip):
        high = table.astype(jnp.bfloat16)
        tables += [high, (table - high.astype(np.float32)).astype(jnp.bfloat16)]
    return np.stack(tables)


def split(value):
    high = value.astype(jnp.bfloat16)
    return high, (value - high.astype(jnp.float32)).astype(jnp.bfloat16)


def mul(left, right):
    return jnp.dot(left, right, preferred_element_type=jnp.float32)


def left_product(high, low, value):
    first, second = split(value)
    return mul(high, first) + (mul(high, second) + mul(low, first))


def right_product(value, high, low):
    first, second = split(value)
    return mul(first, high) + (mul(second, high) + mul(first, low))


def lanes(shape):
    return lax.broadcasted_iota(jnp.int32, shape, 1)


def pack(real, imag):
    half = real.shape[1] // 2
    first = lanes(real.shape) < half
    low = jnp.where(first, real, pltpu.roll(imag, half, 1))
    high = jnp.where(first, pltpu.roll(real, half, 1), imag)
    return low, high


def unpack(low, high):
    half = low.shape[1] // 2
    first = lanes(low.shape) < half
    real = jnp.where(first, low, pltpu.roll(high, half, 1))
    imag = jnp.where(first, pltpu.roll(low, half, 1), high)
    return real, imag


def grow_rows(term, skew):
    count, width = term.shape
    tiles = count // TILE
    sub = lax.broadcasted_iota(jnp.int32, (tiles, TILE, width), 1)
    turned = pltpu.roll(term.reshape(tiles, TILE, width), skew, 1)
    late = jnp.where(sub < skew, turned, 0.0)
    soon = jnp.where(sub < skew, 0.0, turned)
    blank = jnp.zeros((1, TILE, width), jnp.float32)
    grown = jnp.concatenate([soon, blank], 0) + jnp.concatenate([blank, late], 0)
    return grown.reshape(count + TILE, width)


def lane_turn(col, width):
    return jnp.where(col < 0, col + width, col)


class Spot:
    def __init__(self):
        row, col = lax.axis_index("row"), lax.axis_index("col")
        self.side = lax.rem(col, 2)
        self.odd = self.side != 0
        self.row_side = lax.rem(row, 2)
        self.odd_row = self.row_side != 0
        self.has_above = row != 0
        self.has_below = row != lax.axis_size("row") - 1
        self.has_far = (col != 0) & (col != lax.axis_size("col") - 1)


def first_kernel(tile, offsets, counts, first, second, meta, offsets_here, counts_here, sems):
    spot = Spot()
    side = tile.shape[1]
    steps, _, slots = offsets.shape
    near_edge = pl.multiple_of(spot.row_side * RIM, RIM)
    copies = [
        pltpu.make_async_copy(offsets, offsets_here, sems.at[0]),
        pltpu.make_async_copy(counts, counts_here, sems.at[1]),
    ]
    for part in range(2):
        rows = pl.ds(part * RIM, RIM)
        lower = pl.ds(side - RIM - near_edge, RIM)
        upper = pl.ds(near_edge, RIM)
        copies.append(pltpu.make_async_copy(tile.at[part, lower], first.at[rows], sems.at[2 + part]))
        copies.append(pltpu.make_async_copy(tile.at[part, upper], second.at[rows], sems.at[4 + part]))
    for copy in copies:
        copy.start()
    meta[...] = jnp.zeros_like(meta)
    for copy in copies[:2]:
        copy.wait()
    for step in range(steps):
        meta[3 * step : 3 * step + 2, :slots] = offsets_here[step].astype(jnp.float32)
        count = counts_here[:, step : step + 1].astype(jnp.float32)
        meta[3 * step + 2 : 3 * step + 3] = jnp.broadcast_to(count, (1, meta.shape[1]))
    first[2 * RIM :] = meta[...]
    second[2 * RIM :] = meta[...]
    for copy in copies[2:]:
        copy.wait()


def strips_kernel(tile, meta, first, second, tall, near, far):
    side = tile.shape[1]
    spot = Spot()
    odd, odd_row = spot.odd, spot.odd_row
    above = jnp.where(spot.has_above, jnp.where(odd_row, first[...], second[...]), 0.0)
    below = jnp.where(spot.has_below, jnp.where(odd_row, second[...], first[...]), 0.0)
    for part in range(2):
        tall[part, :RIM] = above[part * RIM : (part + 1) * RIM]
        tall[part, RIM : RIM + side] = tile[part]
        tall[part, RIM + side :] = below[part * RIM : (part + 1) * RIM]
    low, high = pack(tall[0], tall[1])
    rows = low.shape[0]
    near[:rows] = jnp.where(odd, low, high)
    far[:rows] = jnp.where(odd, high, low)
    for out in (near, far):
        out[rows : rows + TILE] = above[2 * RIM :]
        out[rows + TILE : rows + 2 * TILE] = meta[...]
        out[rows + 2 * TILE :] = below[2 * RIM :]


def slots_kernel(
    scan, tall, near, far, probe, amps, tables,
    core_out, far_out, keep_out, tall_out, field, sums, totals, wins, psis, starts, sem, *, step,
):
    fetch = pltpu.make_async_copy(scan, starts, sem)
    fetch.start()
    spot = Spot()
    width = probe.shape[1]
    rows_all = tall.shape[1]
    tiles = width // TILE
    slots = amps.shape[0]
    odd = spot.odd
    lane = lanes((width + TILE, width))
    sub = lax.broadcasted_iota(jnp.int32, (tiles, TILE, width), 1)
    from_near, from_far = near[:rows_all], jnp.where(spot.has_far, far[:rows_all], 0.0)
    sides = unpack(jnp.where(odd, from_far, from_near), jnp.where(odd, from_near, from_far))
    for part in range(2):
        field[part, :rows_all, :width] = tall[part]
        field[part, :rows_all, width:] = sides[part]
        field[part, rows_all:] = jnp.zeros_like(field[part, rows_all:])
    sums[...] = jnp.zeros_like(sums)
    fetch.wait()
    full_h, full_l, flip_h, flip_l = (tables[k] for k in range(4))
    pro_r, pro_i = probe[0], probe[1]

    def where(slot):
        row = starts[3 * step, slot] + RIM
        col = starts[3 * step + 1, slot]
        base = pl.multiple_of(row // TILE * TILE, TILE)
        outside = (lane < col) | (lane >= width + col)
        return pl.ds(base, width + TILE), row - base, col, outside

    total = None
    members = range(slots)
    columns = []
    for slot in members:
        rows, skew, col, outside = where(slot)
        lift = jnp.where(skew > 0, TILE - skew, 0)
        back = lane_turn(-col, width)
        win = []
        for part in range(2):
            mixed = jnp.where(outside, field[part, rows, width:], field[part, rows, :width])
            turned = pltpu.roll(mixed.reshape(tiles + 1, TILE, width), lift, 1)
            lined = jnp.where(sub < TILE - skew, turned[:-1], turned[1:])
            win.append(pltpu.roll(lined.reshape(width, width), back, 1))
            wins[slot, part] = win[part]
        psi_r = pro_r * win[0] - pro_i * win[1]
        psi_i = pro_r * win[1] + pro_i * win[0]
        psis[slot, 0] = psi_r
        psis[slot, 1] = psi_i
        columns.append(jnp.concatenate([psi_r, psi_i], 0))

    def turn(half):
        return jnp.concatenate(
            [
                jnp.concatenate(
                    [half[:width, k * width : (k + 1) * width], half[width:, k * width : (k + 1) * width]], 1
                )
                for k in range(slots)
            ],
            0,
        )

    half = left_product(full_h, full_l, jnp.concatenate(columns, 1))
    wave = right_product(turn(half), flip_h, flip_l)
    columns = []
    for k, slot in enumerate(members):
        far_r, far_i = wave[k * width : (k + 1) * width, :width], wave[k * width : (k + 1) * width, width:]
        factor = amps[slot] * lax.rsqrt(jnp.maximum(far_r * far_r + far_i * far_i, 1.0))
        columns.append(jnp.concatenate([far_r * factor, far_i * factor], 0))
    half = left_product(flip_h, flip_l, jnp.concatenate(columns, 1))
    wave = right_product(turn(half), full_h, full_l)
    for k, slot in enumerate(members):
        rows, skew, col, outside = where(slot)
        ahead = lane_turn(col, width)
        live = jnp.where(slot < starts[3 * step + 2, 0], 1.0, 0.0).astype(jnp.float32)
        win_r, win_i = wins[slot, 0], wins[slot, 1]
        chi_r = (wave[k * width : (k + 1) * width, :width] - psis[slot, 0]) * live
        chi_i = (wave[k * width : (k + 1) * width, width:] - psis[slot, 1]) * live

        def deposit(part, term):
            grown = grow_rows(pltpu.roll(term, ahead, 1), skew)
            sums[part, rows, :width] += jnp.where(outside, 0.0, grown)
            sums[part, rows, width:] += jnp.where(outside, grown, 0.0)

        deposit(0, pro_r * chi_r + pro_i * chi_i)
        deposit(1, pro_r * chi_i - pro_i * chi_r)
        terms = (
            win_r * chi_r + win_i * chi_i,
            win_r * chi_i - win_i * chi_r,
            (win_r * win_r + win_i * win_i) * live,
        )
        total = terms if total is None else tuple(a + b for a, b in zip(total, terms))
    half = width // 2
    for part in range(3):
        totals[part] = total[part]
    kept = pl.ds(pl.multiple_of(spot.side * half, half), half)
    given = pl.ds(pl.multiple_of((1 - spot.side) * half, half), half)
    for part in range(3):
        keep_out[part * half : (part + 1) * half] = totals[part, kept]
        core_out[part * half : (part + 1) * half] = totals[part, given]
    for part in range(2):
        tall_out[part] = sums[part, :rows_all, :width]
    low, high = pack(sums[0, :rows_all, width:], sums[1, :rows_all, width:])
    core_out[3 * half :] = jnp.where(odd, high, low)
    far_out[...] = jnp.where(odd, low, high)


def folded(spot, tall, near, far):
    start = near.shape[0] - tall.shape[1]
    odd = spot.odd
    from_near, from_far = near[start:], jnp.where(spot.has_far, far[...], 0.0)
    extra = unpack(jnp.where(odd, from_near, from_far), jnp.where(odd, from_far, from_near))
    return tall[0] + extra[0], tall[1] + extra[1]


def fold_kernel(tall, near, far, first, second):
    rows = first.shape[1]
    spot = Spot()
    odd_row = spot.odd_row
    whole = folded(spot, tall, near, far)
    for part in range(2):
        up, down = whole[part][:rows], whole[part][rows:]
        first[part] = jnp.where(odd_row, up, down)
        second[part] = jnp.where(odd_row, down, up)


def last_fold_kernel(tall, near, far, middle, first, second):
    rows = middle.shape[1]
    spot = Spot()
    odd_row = spot.odd_row
    whole = folded(spot, tall, near, far)
    for part in range(2):
        up, down = whole[part][:RIM], whole[part][RIM + rows :]
        middle[part] = whole[part][RIM : RIM + rows]
        first[part] = jnp.where(odd_row, up, down)
        second[part] = jnp.where(odd_row, down, up)


def weight_kernel(metas, probe, out, spread, *, step, slots):
    width = probe.shape[1]
    lane = lanes((width + TILE, width))
    spread[...] = jnp.zeros_like(spread)
    weight = probe[0] * probe[0] + probe[1] * probe[1]
    for index in range(metas.shape[0]):
        count = metas[index, (3 * step + 2) * slots]
        for slot in range(slots):
            row = metas[index, 3 * step * slots + slot] + (RIM + width + (index // 3 - 1) * width)
            col = metas[index, (3 * step + 1) * slots + slot] + (index % 3 - 1) * width

            @pl.when((slot < count) & (col < width) & (col > -width))
            def _():
                base = pl.multiple_of(row // TILE * TILE, TILE)
                turned = pltpu.roll(weight, lane_turn(col, width), 1)
                grown = grow_rows(turned, row - base)
                inside = (lane >= col) & (lane < width + col)
                spread[pl.ds(base, width + TILE)] += jnp.where(inside, grown, 0.0)

    out[...] = spread[width : width + out.shape[0]]


def update_kernel(tall, sent_1, sent_2, got_1, got_2, weight, new_tall, near, far):
    rows = sent_1.shape[1]
    spot = Spot()
    odd, odd_row = spot.odd, spot.odd_row
    for part in range(2):
        up = jnp.where(odd_row, sent_1[part], sent_2[part])
        down = jnp.where(odd_row, sent_2[part], sent_1[part])
        above = jnp.where(odd_row, got_1[part], got_2[part])
        below = jnp.where(odd_row, got_2[part], got_1[part])
        up = up + jnp.where(spot.has_above, above, 0.0)
        down = down + jnp.where(spot.has_below, below, 0.0)
        head = tall[part, :rows] + up / (weight[:rows] + EPS)
        tail = tall[part, rows:] + down / (weight[rows:] + EPS)
        new_tall[part, :RIM] = jnp.where(spot.has_above, head[:RIM], 0.0)
        new_tall[part, RIM:rows] = head[RIM:]
        new_tall[part, rows : 2 * rows - RIM] = tail[: rows - RIM]
        new_tall[part, 2 * rows - RIM :] = jnp.where(spot.has_below, tail[rows - RIM :], 0.0)
    low, high = pack(new_tall[0], new_tall[1])
    near[...] = jnp.where(odd, low, high)
    far[...] = jnp.where(odd, high, low)


def last_kernel(tall, middle, got_1, got_2, weight, tile):
    side = tile.shape[1]
    spot = Spot()
    odd_row = spot.odd_row
    for part in range(2):
        above = jnp.where(odd_row, got_1[part], got_2[part])
        below = jnp.where(odd_row, got_2[part], got_1[part])
        above = jnp.where(spot.has_above, above, 0.0)
        below = jnp.where(spot.has_below, below, 0.0)
        num = middle[part] + jnp.concatenate([above, below], 0)
        tile[part] = tall[part, RIM : RIM + side] + num / (weight[RIM : RIM + side] + EPS)


def call(kernel, shapes, places, operands, flops=1000000, moved=MIB, scratch=(), more=(), limit=16):
    vmem = pl.BlockSpec(memory_space=pltpu.VMEM)
    smem = pl.BlockSpec(memory_space=pltpu.SMEM)
    anywhere = pl.BlockSpec(memory_space=pl.ANY)
    return pl.pallas_call(
        kernel,
        out_shape=tuple(jax.ShapeDtypeStruct(shape, jnp.float32) for shape in shapes),
        in_specs=[{"s": smem, "a": anywhere}.get(where, vmem) for where in places.ljust(len(operands), "v")],
        out_specs=tuple(vmem for _ in shapes),
        scratch_shapes=[pltpu.VMEM(shape, jnp.float32) for shape in scratch] + list(more),
        compiler_params=pltpu.CompilerParams(vmem_limit_bytes=limit * MIB),
        cost_estimate=pl.CostEstimate(flops=flops, bytes_accessed=moved, transcendentals=0),
    )(*operands)


def swap(value, axis, bit):
    return lax.ppermute(value, axis, [(i, i ^ bit) for i in range(lax.axis_size(axis))])


def swap_far(value):
    rows, cols = lax.axis_size("row"), lax.axis_size("col")
    pairs = []
    for row in range(rows):
        for col in range(cols):
            to_row, to_col = row, col + (1 if col % 2 else -1)
            if not 0 <= to_col < cols:
                to_row, to_col = row ^ 1, col
            pairs.append((row * cols + col, to_row * cols + to_col))
    return lax.ppermute(value, AXES, pairs)


def swap_rows(value):
    rows, cols = lax.axis_size("row"), lax.axis_size("col")
    pairs = []
    for row in range(rows):
        for col in range(cols):
            to_row, to_col = row + (1 if row % 2 else -1), col
            if not 0 <= to_row < rows:
                to_row, to_col = row, col ^ 1
            pairs.append((row * cols + col, to_row * cols + to_col))
    return lax.ppermute(value, AXES, pairs)


def after(*values):
    return lax.optimization_barrier(values)


def chip_steps():
    steps = [("row", 1)]
    for axis in ("col", "row"):
        bit = 2
        while bit < lax.axis_size(axis):
            steps.append((axis, bit))
            bit *= 2
    return steps


def add_step(part, step):
    return part + swap(part, *step)


def body(object_field, probe, positions, counts, amplitude):
    side = object_field.shape[1]
    width = probe.shape[1]
    half = width // 2
    steps = positions.shape[2]
    slots = positions.shape[3]
    tall_rows = side + 2 * RIM
    row, col = lax.axis_index("row"), lax.axis_index("col")
    odd, odd_row = col % 2, row % 2
    outer = (col == 0) | (col == lax.axis_size("col") - 1)
    tables = jnp.asarray(dft_tables(width))

    offsets = jnp.swapaxes(positions[0, 0], 1, 2)
    flat = 2 * RIM
    first, second, meta = call(
        first_kernel,
        ((flat + TILE, width), (flat + TILE, width), (TILE, width)),
        "aaa",
        (object_field, offsets, counts[0]),
        more=(
            pltpu.VMEM(offsets.shape, jnp.int32),
            pltpu.VMEM((1, steps), jnp.int32),
            pltpu.SemaphoreType.DMA((6,)),
        ),
        limit=60,
    )
    scan = meta[: 3 * steps, :slots].astype(jnp.int32)
    first, second = swap(first, "row", 1), swap_rows(second)
    strip = (tall_rows + 3 * TILE, width)
    tall, near, far = call(
        strips_kernel,
        ((2, tall_rows, side), strip, strip),
        "",
        (object_field, meta, first, second),
    )
    near, far = swap(near, "col", 1), swap_far(far)

    def three(value):
        return value[tall_rows:].reshape(3, TILE, width)[:, : 3 * steps, :slots]

    above = jnp.where(row > 0, jnp.where(odd_row != 0, first[flat:], second[flat:]), 0.0)
    below = jnp.where(row < lax.axis_size("row") - 1, jnp.where(odd_row != 0, second[flat:], first[flat:]), 0.0)
    here = jnp.stack([above, meta, below])[:, : 3 * steps, :slots]
    sides = three(near), jnp.where(outer, 0.0, three(far))
    left = jnp.where(odd != 0, sides[0], sides[1])
    right = jnp.where(odd != 0, sides[1], sides[0])
    metas = jnp.stack([left, here, right], 1).reshape(9, -1).astype(jnp.int32)

    current = probe
    for step in range(steps):
        core, out_far, kept, sums = call(
            functools.partial(slots_kernel, step=step),
            (
                (3 * half + tall_rows, width),
                (tall_rows, width),
                (3 * half, width),
                (2, tall_rows, width),
            ),
            "a",
            (scan, tall, near, far, current, amplitude[0, 0, step], tables),
            flops=slots * 96 * width * width * width,
            moved=4 * MIB,
            scratch=(
                (2, tall_rows + TILE, 2 * width),
                (2, tall_rows + TILE, 2 * width),
                (3, width, width),
                (slots, 2, width, width),
                (slots, 2, width, width),
            ),
            more=(pltpu.SMEM(scan.shape, jnp.int32), pltpu.SemaphoreType.DMA(())),
            limit=24,
        )
        core = swap(core, "col", 1)
        out_far = swap_far(out_far)
        last = step == steps - 1
        first_step, second_step, *others, last_step = chip_steps()
        part = add_step(kept + core[: 3 * half], first_step)
        (weight,) = call(
            functools.partial(weight_kernel, step=step, slots=slots),
            ((tall_rows, width),),
            "s",
            (metas, current),
            scratch=((tall_rows + 2 * width + TILE, width),),
        )
        part, weight = after(part, weight)
        part = add_step(part, second_step)
        if last:
            middle, sent_1, sent_2 = call(
                last_fold_kernel,
                ((2, side, width), (2, RIM, width), (2, RIM, width)),
                "",
                (sums, core, out_far),
            )
        else:
            sent_1, sent_2 = call(
                fold_kernel,
                ((2, tall_rows // 2, width), (2, tall_rows // 2, width)),
                "",
                (sums, core, out_far),
            )
        got_1, got_2 = swap(sent_1, "row", 1), swap_rows(sent_2)
        for other_step in others:
            part = add_step(part, other_step)
        if last:
            (tile,) = call(
                last_kernel,
                ((2, side, side),),
                "",
                (tall, middle, got_1, got_2, weight),
            )
            part = add_step(part, last_step)
        else:
            tall, near, far = call(
                update_kernel,
                ((2, tall_rows, side), (tall_rows, width), (tall_rows, width)),
                "",
                (tall, sent_1, sent_2, got_1, got_2, weight),
            )
            far_1, far_2 = swap_far(far[: tall_rows // 2]), swap_far(far[tall_rows // 2 :])
            part = add_step(part, last_step)
            part, far_1, far_2 = after(part, far_1, far_2)
            far = jnp.concatenate([far_1, far_2], 0)
        mine = lax.dynamic_slice_in_dim(current, odd * half, half, 1)
        part = part.reshape(3, half, width)
        mine = mine + part[:2] / (part[2] + EPS)[None]
        if last:
            other = swap(mine, "col", 1)
        else:
            near = swap(jnp.concatenate([near, mine.reshape(2 * half, width)], 0), "col", 1)
            other = near[tall_rows:].reshape(2, half, width)
        low = jnp.where(odd == 0, mine, other)
        high = jnp.where(odd == 0, other, mine)
        current = jnp.concatenate([low, high], 1)
    return (tile, current)


def solution(mesh):
    return jax.shard_map(
        body,
        mesh=mesh,
        in_specs=(
            P(None, "row", "col"),
            P(),
            P("row", "col", None, None, None),
            P("row", "col", None),
            P("row", "col", None, None, None, None),
        ),
        out_specs=(P(None, "row", "col"), P()),
        check_vma=False,
    )
```

```python
import functools
import math

import jax
import jax.numpy as jnp
import numpy as np
from jax import lax
from jax.experimental import pallas as pl
from jax.experimental.pallas import tpu as pltpu
from jax.sharding import PartitionSpec as P

RIM = 64
TILE = 8
EPS = 0.1
AXES = ("row", "col")
MIB = 1024 * 1024


def dft_tables(size):
    index = np.arange(size)
    angle = (index[:, None] * index[None, :] % size) * (-2.0 * math.pi / size)
    cosine = np.cos(angle) / math.sqrt(size)
    sine = np.sin(angle) / math.sqrt(size)
    full = np.block([[cosine, -sine], [sine, cosine]]).astype(np.float32)
    flip = np.ascontiguousarray(full.T)
    tables = []
    for table in (full, flip):
        high = table.astype(jnp.bfloat16)
        tables += [high, (table - high.astype(np.float32)).astype(jnp.bfloat16)]
    return np.stack(tables)


def split(value):
    high = value.astype(jnp.bfloat16)
    return high, (value - high.astype(jnp.float32)).astype(jnp.bfloat16)


def mul(left, right):
    return jnp.dot(left, right, preferred_element_type=jnp.float32)


def left_product(high, low, value):
    first, second = split(value)
    return mul(high, first) + (mul(high, second) + mul(low, first))


def right_product(value, high, low):
    first, second = split(value)
    return mul(first, high) + (mul(second, high) + mul(first, low))


def lanes(shape):
    return lax.broadcasted_iota(jnp.int32, shape, 1)


def pack(real, imag):
    half = real.shape[1] // 2
    first = lanes(real.shape) < half
    low = jnp.where(first, real, pltpu.roll(imag, half, 1))
    high = jnp.where(first, pltpu.roll(real, half, 1), imag)
    return low, high


def unpack(low, high):
    half = low.shape[1] // 2
    first = lanes(low.shape) < half
    real = jnp.where(first, low, pltpu.roll(high, half, 1))
    imag = jnp.where(first, pltpu.roll(low, half, 1), high)
    return real, imag


def grow_rows(term, skew):
    count, width = term.shape
    tiles = count // TILE
    sub = lax.broadcasted_iota(jnp.int32, (tiles, TILE, width), 1)
    turned = pltpu.roll(term.reshape(tiles, TILE, width), skew, 1)
    late = jnp.where(sub < skew, turned, 0.0)
    soon = jnp.where(sub < skew, 0.0, turned)
    blank = jnp.zeros((1, TILE, width), jnp.float32)
    grown = jnp.concatenate([soon, blank], 0) + jnp.concatenate([blank, late], 0)
    return grown.reshape(count + TILE, width)


def lane_turn(col, width):
    return jnp.where(col < 0, col + width, col)


class Plain:
    def __init__(self, value):
        self.value = value

    def __getitem__(self, where):
        row, col = where
        return self.value[row, col]


class Spot:
    def __init__(self):
        row, col = lax.axis_index("row"), lax.axis_index("col")
        self.side = lax.rem(col, 2)
        self.odd = self.side != 0
        self.row_side = lax.rem(row, 2)
        self.odd_row = self.row_side != 0
        self.has_above = row != 0
        self.has_below = row != lax.axis_size("row") - 1
        self.has_far = (col != 0) & (col != lax.axis_size("col") - 1)


def first_kernel(tile, offsets, counts, first, second, meta, offsets_here, counts_here, sems):
    spot = Spot()
    side = tile.shape[1]
    steps, _, slots = offsets.shape
    near_edge = pl.multiple_of(spot.row_side * RIM, RIM)
    copies = [
        pltpu.make_async_copy(offsets, offsets_here, sems.at[0]),
        pltpu.make_async_copy(counts, counts_here, sems.at[1]),
    ]
    for part in range(2):
        rows = pl.ds(part * RIM, RIM)
        lower = pl.ds(side - RIM - near_edge, RIM)
        upper = pl.ds(near_edge, RIM)
        copies.append(pltpu.make_async_copy(tile.at[part, lower], first.at[rows], sems.at[2 + part]))
        copies.append(pltpu.make_async_copy(tile.at[part, upper], second.at[rows], sems.at[4 + part]))
    for copy in copies:
        copy.start()
    meta[...] = jnp.zeros_like(meta)
    for copy in copies[:2]:
        copy.wait()
    for step in range(steps):
        meta[3 * step : 3 * step + 2, :slots] = offsets_here[step].astype(jnp.float32)
        count = counts_here[:, step : step + 1].astype(jnp.float32)
        meta[3 * step + 2 : 3 * step + 3] = jnp.broadcast_to(count, (1, meta.shape[1]))
    first[2 * RIM :] = meta[...]
    second[2 * RIM :] = meta[...]
    for copy in copies[2:]:
        copy.wait()


def strips_kernel(tile, meta, first, second, tall, near, far):
    side = tile.shape[1]
    spot = Spot()
    odd, odd_row = spot.odd, spot.odd_row
    above = jnp.where(spot.has_above, jnp.where(odd_row, first[...], second[...]), 0.0)
    below = jnp.where(spot.has_below, jnp.where(odd_row, second[...], first[...]), 0.0)
    for part in range(2):
        tall[part, :RIM] = above[part * RIM : (part + 1) * RIM]
        tall[part, RIM : RIM + side] = tile[part]
        tall[part, RIM + side :] = below[part * RIM : (part + 1) * RIM]
    low, high = pack(tall[0], tall[1])
    rows = low.shape[0]
    near[:rows] = jnp.where(odd, low, high)
    far[:rows] = jnp.where(odd, high, low)
    for out in (near, far):
        out[rows : rows + TILE] = above[2 * RIM :]
        out[rows + TILE : rows + 2 * TILE] = meta[...]
        out[rows + 2 * TILE :] = below[2 * RIM :]


def window_place(starts, step, slot, width):
    row = starts[3 * step, slot] + RIM
    col = starts[3 * step + 1, slot]
    base = pl.multiple_of(row // TILE * TILE, TILE)
    lane = lanes((width + TILE, width))
    outside = (lane < col) | (lane >= width + col)
    return pl.ds(base, width + TILE), row - base, col, outside


def take_windows(starts, field, wins, weight, step):
    slots, _, width, _ = wins.shape
    tiles = width // TILE
    sub = lax.broadcasted_iota(jnp.int32, (tiles, TILE, width), 1)
    total = None
    for slot in range(slots):
        rows, skew, col, outside = window_place(starts, step, slot, width)
        live = jnp.where(slot < starts[3 * step + 2, 0], 1.0, 0.0).astype(jnp.float32)
        lift = jnp.where(skew > 0, TILE - skew, 0)
        back = lane_turn(-col, width)
        power = None
        for part in range(2):
            mixed = jnp.where(outside, field[part, rows, width:], field[part, rows, :width])
            turned = pltpu.roll(mixed.reshape(tiles + 1, TILE, width), lift, 1)
            lined = jnp.where(sub < TILE - skew, turned[:-1], turned[1:])
            win = pltpu.roll(lined.reshape(width, width), back, 1)
            wins[slot, part] = win
            power = win * win if power is None else power + win * win
        total = power * live if total is None else total + power * live
    weight[...] = total


def field_kernel(scan, tall, near, far, wins, weight, field, *, step):
    spot = Spot()
    width = tall.shape[2]
    rows = tall.shape[1]
    from_near, from_far = near[:rows], jnp.where(spot.has_far, far[:rows], 0.0)
    sides = unpack(
        jnp.where(spot.odd, from_far, from_near), jnp.where(spot.odd, from_near, from_far)
    )
    for part in range(2):
        field[part, :rows, :width] = tall[part]
        field[part, :rows, width:] = sides[part]
        field[part, rows:] = jnp.zeros_like(field[part, rows:])
    starts = Plain(scan[...])
    take_windows(starts, field, wins, weight, step)


def slots_kernel(
    scan, wins, win_weight, probe, amps, tables,
    core_out, far_out, keep_out, sums_out, sums, totals, psis, *, step,
):
    starts = Plain(scan[...])
    spot = Spot()
    width = probe.shape[1]
    rows_all = sums_out.shape[1]
    slots = amps.shape[0]
    odd = spot.odd
    sums[...] = jnp.zeros_like(sums)
    full_h, full_l, flip_h, flip_l = (tables[k] for k in range(4))
    pro_r, pro_i = probe[0], probe[1]
    columns = []
    for slot in range(slots):
        psi_r = pro_r * wins[slot, 0] - pro_i * wins[slot, 1]
        psi_i = pro_r * wins[slot, 1] + pro_i * wins[slot, 0]
        psis[slot, 0] = psi_r
        psis[slot, 1] = psi_i
        columns.append(jnp.concatenate([psi_r, psi_i], 0))

    def block(value, k):
        return value[k * width : (k + 1) * width]

    def turn(half):
        parts = []
        for k in range(slots):
            both = half[:, k * width : (k + 1) * width]
            parts.append(jnp.concatenate([both[:width], both[width:]], 1))
        return jnp.concatenate(parts, 0)

    half = left_product(full_h, full_l, jnp.concatenate(columns, 1))
    wave = right_product(turn(half), flip_h, flip_l)
    columns = []
    for slot in range(slots):
        far_r, far_i = block(wave, slot)[:, :width], block(wave, slot)[:, width:]
        factor = amps[slot] * lax.rsqrt(jnp.maximum(far_r * far_r + far_i * far_i, 1.0))
        columns.append(jnp.concatenate([far_r * factor, far_i * factor], 0))
    half = left_product(flip_h, flip_l, jnp.concatenate(columns, 1))
    wave = right_product(turn(half), full_h, full_l)
    total = None
    for slot in range(slots):
        rows, skew, col, outside = window_place(starts, step, slot, width)
        ahead = lane_turn(col, width)
        live = jnp.where(slot < starts[3 * step + 2, 0], 1.0, 0.0).astype(jnp.float32)
        win_r, win_i = wins[slot, 0], wins[slot, 1]
        chi_r = (block(wave, slot)[:, :width] - psis[slot, 0]) * live
        chi_i = (block(wave, slot)[:, width:] - psis[slot, 1]) * live

        def deposit(part, term):
            grown = grow_rows(pltpu.roll(term, ahead, 1), skew)
            sums[part, rows, :width] += jnp.where(outside, 0.0, grown)
            sums[part, rows, width:] += jnp.where(outside, grown, 0.0)

        deposit(0, pro_r * chi_r + pro_i * chi_i)
        deposit(1, pro_r * chi_i - pro_i * chi_r)
        terms = (win_r * chi_r + win_i * chi_i, win_r * chi_i - win_i * chi_r)
        total = terms if total is None else tuple(a + b for a, b in zip(total, terms))
    half = width // 2
    totals[0], totals[1], totals[2] = total[0], total[1], win_weight[...]
    kept = pl.ds(pl.multiple_of(spot.side * half, half), half)
    given = pl.ds(pl.multiple_of((1 - spot.side) * half, half), half)
    for part in range(3):
        keep_out[part * half : (part + 1) * half] = totals[part, kept]
        core_out[part * half : (part + 1) * half] = totals[part, given]
    for part in range(2):
        sums_out[part] = sums[part, :rows_all, :width]
    low, high = pack(sums[0, :rows_all, width:], sums[1, :rows_all, width:])
    core_out[3 * half :] = jnp.where(odd, high, low)
    far_out[...] = jnp.where(odd, low, high)


def folded(spot, tall, near, far):
    start = near.shape[0] - tall.shape[1]
    odd = spot.odd
    from_near, from_far = near[start:], jnp.where(spot.has_far, far[...], 0.0)
    extra = unpack(jnp.where(odd, from_near, from_far), jnp.where(odd, from_far, from_near))
    return tall[0] + extra[0], tall[1] + extra[1]


def fold_kernel(tall, near, far, first, second):
    rows = first.shape[1]
    spot = Spot()
    odd_row = spot.odd_row
    whole = folded(spot, tall, near, far)
    for part in range(2):
        up, down = whole[part][:rows], whole[part][rows:]
        first[part] = jnp.where(odd_row, up, down)
        second[part] = jnp.where(odd_row, down, up)


def last_fold_kernel(tall, near, far, middle, first, second):
    rows = middle.shape[1]
    spot = Spot()
    odd_row = spot.odd_row
    whole = folded(spot, tall, near, far)
    for part in range(2):
        up, down = whole[part][:RIM], whole[part][RIM + rows :]
        middle[part] = whole[part][RIM : RIM + rows]
        first[part] = jnp.where(odd_row, up, down)
        second[part] = jnp.where(odd_row, down, up)


def weight_kernel(metas, probe, out, spread, *, step, slots):
    width = probe.shape[1]
    lane = lanes((width + TILE, width))
    spread[...] = jnp.zeros_like(spread)
    weight = probe[0] * probe[0] + probe[1] * probe[1]
    for index in range(metas.shape[0]):
        count = metas[index, (3 * step + 2) * slots]
        for slot in range(slots):
            row = metas[index, 3 * step * slots + slot] + (RIM + width + (index // 3 - 1) * width)
            col = metas[index, (3 * step + 1) * slots + slot] + (index % 3 - 1) * width

            base = pl.multiple_of(row // TILE * TILE, TILE)
            grown = grow_rows(pltpu.roll(weight, lax.rem(col + 2 * width, width), 1), row - base)
            edge = jnp.where(slot < count, col, 2 * width)
            inside = (lane >= edge) & (lane < width + edge)
            spread[pl.ds(base, width + TILE)] += jnp.where(inside, grown, 0.0)

    out[...] = spread[width : width + out.shape[0]]


def update_kernel(tall, sent_1, sent_2, got_1, got_2, weight, _, new_tall, near, far):
    rows = sent_1.shape[1]
    spot = Spot()
    odd, odd_row = spot.odd, spot.odd_row
    for part in range(2):
        up = jnp.where(odd_row, sent_1[part], sent_2[part])
        down = jnp.where(odd_row, sent_2[part], sent_1[part])
        above = jnp.where(odd_row, got_1[part], got_2[part])
        below = jnp.where(odd_row, got_2[part], got_1[part])
        up = up + jnp.where(spot.has_above, above, 0.0)
        down = down + jnp.where(spot.has_below, below, 0.0)
        head = tall[part, :rows] + up / (weight[:rows] + EPS)
        tail = tall[part, rows:] + down / (weight[rows:] + EPS)
        new_tall[part, :RIM] = jnp.where(spot.has_above, head[:RIM], 0.0)
        new_tall[part, RIM:rows] = head[RIM:]
        new_tall[part, rows : 2 * rows - RIM] = tail[: rows - RIM]
        new_tall[part, 2 * rows - RIM :] = jnp.where(spot.has_below, tail[rows - RIM :], 0.0)
    low, high = pack(new_tall[0], new_tall[1])
    near[...] = jnp.where(odd, low, high)
    far[...] = jnp.where(odd, high, low)


def last_kernel(tall, middle, got_1, got_2, weight, tile):
    side = tile.shape[1]
    spot = Spot()
    odd_row = spot.odd_row
    for part in range(2):
        above = jnp.where(odd_row, got_1[part], got_2[part])
        below = jnp.where(odd_row, got_2[part], got_1[part])
        above = jnp.where(spot.has_above, above, 0.0)
        below = jnp.where(spot.has_below, below, 0.0)
        num = middle[part] + jnp.concatenate([above, below], 0)
        tile[part] = tall[part, RIM : RIM + side] + num / (weight[RIM : RIM + side] + EPS)


def call(kernel, shapes, places, operands, flops=1000000, moved=MIB, scratch=(), more=(), limit=16):
    vmem = pl.BlockSpec(memory_space=pltpu.VMEM)
    smem = pl.BlockSpec(memory_space=pltpu.SMEM)
    anywhere = pl.BlockSpec(memory_space=pl.ANY)
    return pl.pallas_call(
        kernel,
        out_shape=tuple(jax.ShapeDtypeStruct(shape, jnp.float32) for shape in shapes),
        in_specs=[{"s": smem, "a": anywhere}.get(where, vmem) for where in places.ljust(len(operands), "v")],
        out_specs=tuple(vmem for _ in shapes),
        scratch_shapes=[pltpu.VMEM(shape, jnp.float32) for shape in scratch] + list(more),
        compiler_params=pltpu.CompilerParams(vmem_limit_bytes=limit * MIB),
        cost_estimate=pl.CostEstimate(flops=flops, bytes_accessed=moved, transcendentals=0),
    )(*operands)


def swap(value, axis, bit):
    return lax.ppermute(value, axis, [(i, i ^ bit) for i in range(lax.axis_size(axis))])


def swap_far(value):
    rows, cols = lax.axis_size("row"), lax.axis_size("col")
    pairs = []
    for row in range(rows):
        for col in range(cols):
            to_row, to_col = row, col + (1 if col % 2 else -1)
            if not 0 <= to_col < cols:
                to_row, to_col = row ^ 1, col
            pairs.append((row * cols + col, to_row * cols + to_col))
    return lax.ppermute(value, AXES, pairs)


def swap_rows(value):
    rows, cols = lax.axis_size("row"), lax.axis_size("col")
    pairs = []
    for row in range(rows):
        for col in range(cols):
            to_row, to_col = row + (1 if row % 2 else -1), col
            if not 0 <= to_row < rows:
                to_row, to_col = row, col ^ 1
            pairs.append((row * cols + col, to_row * cols + to_col))
    return lax.ppermute(value, AXES, pairs)


def after(*values):
    return lax.optimization_barrier(values)


def chip_steps():
    steps = [("row", 1)]
    for axis in ("col", "row"):
        bit = 2
        while bit < lax.axis_size(axis):
            steps.append((axis, bit))
            bit *= 2
    return steps


def swap_both(value):
    rows, cols = lax.axis_size("row"), lax.axis_size("col")
    pairs = [(r * cols + c, (r ^ 1) * cols + (c ^ 2)) for r in range(rows) for c in range(cols)]
    return lax.ppermute(value, AXES, pairs)


def chain_steps():
    return lax.axis_size("row").bit_length() - 2


def add_plane(part, weight):
    part_y, part_x, part_xy = swap(part, "row", 1), swap(part, "col", 2), swap_both(part)
    if weight is not None:
        part_xy, weight = after(part_xy, weight)
    return (part + part_y) + (part_x + part_xy)


def add_step(part, step):
    return part + swap(part, *step)


def body(object_field, probe, positions, counts, amplitude):
    side = object_field.shape[1]
    width = probe.shape[1]
    half = width // 2
    steps = positions.shape[2]
    slots = positions.shape[3]
    tall_rows = side + 2 * RIM
    row, col = lax.axis_index("row"), lax.axis_index("col")
    odd, odd_row = col % 2, row % 2
    outer = (col == 0) | (col == lax.axis_size("col") - 1)
    tables = jnp.asarray(dft_tables(width))

    offsets = jnp.swapaxes(positions[0, 0], 1, 2)
    flat = 2 * RIM
    first, second, meta = call(
        first_kernel,
        ((flat + TILE, width), (flat + TILE, width), (TILE, width)),
        "aaa",
        (object_field, offsets, counts[0]),
        more=(
            pltpu.VMEM(offsets.shape, jnp.int32),
            pltpu.VMEM((1, steps), jnp.int32),
            pltpu.SemaphoreType.DMA((6,)),
        ),
        limit=60,
    )
    scan = meta[: 3 * steps, :slots].astype(jnp.int32)
    first, second = swap(first, "row", 1), swap_rows(second)
    strip = (tall_rows + 3 * TILE, width)
    tall, near, far = call(
        strips_kernel,
        ((2, tall_rows, side), strip, strip),
        "",
        (object_field, meta, first, second),
    )
    near, far = swap(near, "col", 1), swap_far(far)

    def three(value):
        return value[tall_rows:].reshape(3, TILE, width)[:, : 3 * steps, :slots]

    above = jnp.where(row > 0, jnp.where(odd_row != 0, first[flat:], second[flat:]), 0.0)
    below = jnp.where(row < lax.axis_size("row") - 1, jnp.where(odd_row != 0, second[flat:], first[flat:]), 0.0)
    here = jnp.stack([above, meta, below])[:, : 3 * steps, :slots]
    sides = three(near), jnp.where(outer, 0.0, three(far))
    left = jnp.where(odd != 0, sides[0], sides[1])
    right = jnp.where(odd != 0, sides[1], sides[0])
    metas = jnp.stack([left, here, right], 1).reshape(9, -1).astype(jnp.int32)

    def windows(step, tall, near, far):
        return call(
            functools.partial(field_kernel, step=step),
            ((slots, 2, width, width), (width, width)),
            "",
            (scan, tall, near, far),
            scratch=((2, tall_rows + TILE, 2 * width),),
        )

    wins, win_weight = windows(0, tall, near, far)
    current = probe
    for step in range(steps):
        last = step == steps - 1
        core, out_far, kept, sums = call(
            functools.partial(slots_kernel, step=step),
            (
                (3 * half + tall_rows, width),
                (tall_rows, width),
                (3 * half, width),
                (2, tall_rows, width),
            ),
            "",
            (scan, wins, win_weight, current, amplitude[0, 0, step], tables),
            flops=slots * 96 * width * width * width,
            moved=4 * MIB,
            scratch=(
                (2, tall_rows + TILE, 2 * width),
                (3, width, width),
                (slots, 2, width, width),
            ),
            limit=24,
        )
        core = swap(core, "col", 1)
        out_far = swap_far(out_far)
        (weight,) = call(
            functools.partial(weight_kernel, step=step, slots=slots),
            ((tall_rows, width),),
            "s",
            (metas, current),
            scratch=((tall_rows + 2 * width + TILE, width),),
        )
        part = kept + core[: 3 * half]
        if last:
            middle, sent_1, sent_2 = call(
                last_fold_kernel,
                ((2, side, width), (2, RIM, width), (2, RIM, width)),
                "",
                (sums, core, out_far),
            )
            got_1, got_2 = swap(sent_1, "row", 1), swap_rows(sent_2)
            (tile,) = call(
                last_kernel,
                ((2, side, side),),
                "",
                (tall, middle, got_1, got_2, weight),
            )
            part = add_plane(part, weight)
            for other_step in chip_steps()[-chain_steps() : -1]:
                part = add_step(part, other_step)
            part = add_step(part, chip_steps()[-1])
        else:
            sent_1, sent_2 = call(
                fold_kernel,
                ((2, tall_rows // 2, width), (2, tall_rows // 2, width)),
                "",
                (sums, core, out_far),
            )
            got_1, got_2 = swap(sent_1, "row", 1), swap_rows(sent_2)
            part = add_plane(part, weight)
            for other_step in chip_steps()[-chain_steps() : -1]:
                part = add_step(part, other_step)
            tall, near, far = call(
                update_kernel,
                ((2, tall_rows, side), (tall_rows, width), (tall_rows, width)),
                "",
                (tall, sent_1, sent_2, got_1, got_2, weight, part[:TILE]),
            )
            near = swap(near, "col", 1)
            far_1, far_2 = swap_far(far[: tall_rows // 2]), swap_far(far[tall_rows // 2 :])
            part = add_step(part, chip_steps()[-1])
            far = jnp.concatenate([far_1, far_2], 0)
            wins, win_weight = windows(step + 1, tall, near, far)
        mine = lax.dynamic_slice_in_dim(current, odd * half, half, 1)
        part = part.reshape(3, half, width)
        mine = mine + part[:2] / (part[2] + EPS)[None]
        other = swap(mine, "col", 1)
        low = jnp.where(odd == 0, mine, other)
        high = jnp.where(odd == 0, other, mine)
        current = jnp.concatenate([low, high], 1)
    return (tile, current)


def solution(mesh):
    return jax.shard_map(
        body,
        mesh=mesh,
        in_specs=(
            P(None, "row", "col"),
            P(),
            P("row", "col", None, None, None),
            P("row", "col", None),
            P("row", "col", None, None, None, None),
        ),
        out_specs=(P(None, "row", "col"), P()),
        check_vma=False,
    )
```

```python
import functools
import math

import jax
import jax.numpy as jnp
import numpy as np
from jax import lax
from jax.experimental import pallas as pl
from jax.experimental.pallas import tpu as pltpu
from jax.sharding import PartitionSpec as P

RIM = 64
TILE = 8
EPS = 0.1
AXES = ("row", "col")
MIB = 1024 * 1024


def dft_tables(size):
    index = np.arange(size)
    angle = (index[:, None] * index[None, :] % size) * (-2.0 * math.pi / size)
    cosine = np.cos(angle) / math.sqrt(size)
    sine = np.sin(angle) / math.sqrt(size)
    tables = []
    for table in (cosine.astype(np.float32), sine.astype(np.float32)):
        high = table.astype(jnp.bfloat16)
        low = (table - high.astype(np.float32)).astype(jnp.bfloat16)
        tables += [high, low]
    return np.stack(tables + [-tables[2], -tables[3]])


def split(value):
    high = value.astype(jnp.bfloat16)
    return high, (value - high.astype(jnp.float32)).astype(jnp.bfloat16)


def mul(left, right):
    return jnp.dot(left, right, preferred_element_type=jnp.float32)


def left_product(high, low, value):
    first, second = split(value)
    return mul(high, first) + (mul(high, second) + mul(low, first))


def right_product(value, high, low):
    first, second = split(value)
    return mul(first, high) + (mul(second, high) + mul(first, low))


def lanes(shape):
    return lax.broadcasted_iota(jnp.int32, shape, 1)


def pack(real, imag):
    half = real.shape[1] // 2
    first = lanes(real.shape) < half
    low = jnp.where(first, real, pltpu.roll(imag, half, 1))
    high = jnp.where(first, pltpu.roll(real, half, 1), imag)
    return low, high


def unpack(low, high):
    half = low.shape[1] // 2
    first = lanes(low.shape) < half
    real = jnp.where(first, low, pltpu.roll(high, half, 1))
    imag = jnp.where(first, pltpu.roll(low, half, 1), high)
    return real, imag


def grow_rows(term, skew):
    count, width = term.shape
    tiles = count // TILE
    sub = lax.broadcasted_iota(jnp.int32, (tiles, TILE, width), 1)
    turned = pltpu.roll(term.reshape(tiles, TILE, width), skew, 1)
    late = jnp.where(sub < skew, turned, 0.0)
    soon = jnp.where(sub < skew, 0.0, turned)
    blank = jnp.zeros((1, TILE, width), jnp.float32)
    grown = jnp.concatenate([soon, blank], 0) + jnp.concatenate([blank, late], 0)
    return grown.reshape(count + TILE, width)


def lane_turn(col, width):
    return jnp.where(col < 0, col + width, col)


class Plain:
    def __init__(self, value):
        self.value = value

    def __getitem__(self, where):
        row, col = where
        return self.value[row, col]


class Spot:
    def __init__(self):
        row, col = lax.axis_index("row"), lax.axis_index("col")
        self.side = lax.rem(col, 2)
        self.odd = self.side != 0
        self.row_side = lax.rem(row, 2)
        self.odd_row = self.row_side != 0
        self.has_above = row != 0
        self.has_below = row != lax.axis_size("row") - 1
        self.has_far = (col != 0) & (col != lax.axis_size("col") - 1)


def first_kernel(tile, offsets, counts, first, second, meta, offsets_here, counts_here, sems):
    spot = Spot()
    side = tile.shape[1]
    steps, _, slots = offsets.shape
    near_edge = pl.multiple_of(spot.row_side * RIM, RIM)
    copies = [
        pltpu.make_async_copy(offsets, offsets_here, sems.at[0]),
        pltpu.make_async_copy(counts, counts_here, sems.at[1]),
    ]
    for part in range(2):
        rows = pl.ds(part * RIM, RIM)
        lower = pl.ds(side - RIM - near_edge, RIM)
        upper = pl.ds(near_edge, RIM)
        copies.append(pltpu.make_async_copy(tile.at[part, lower], first.at[rows], sems.at[2 + part]))
        copies.append(pltpu.make_async_copy(tile.at[part, upper], second.at[rows], sems.at[4 + part]))
    for copy in copies:
        copy.start()
    meta[...] = jnp.zeros_like(meta)
    for copy in copies[:2]:
        copy.wait()
    for step in range(steps):
        meta[3 * step : 3 * step + 2, :slots] = offsets_here[step].astype(jnp.float32)
        count = counts_here[:, step : step + 1].astype(jnp.float32)
        meta[3 * step + 2 : 3 * step + 3] = jnp.broadcast_to(count, (1, meta.shape[1]))
    first[2 * RIM :] = meta[...]
    second[2 * RIM :] = meta[...]
    for copy in copies[2:]:
        copy.wait()


def early_kernel(tile, meta, first, far):
    odd = Spot().odd
    side = tile.shape[1]
    for at, real, imag in ((0, first[:RIM], first[RIM : 2 * RIM]), (RIM, tile[0], tile[1])):
        low, high = pack(real, imag)
        far[at : at + low.shape[0]] = jnp.where(odd, high, low)
    far[RIM + side : RIM + side + TILE] = first[2 * RIM :]
    far[RIM + side + TILE :] = meta[...]


def strips_kernel(tile, meta, first, second, tall, near, far):
    side = tile.shape[1]
    spot = Spot()
    odd, odd_row = spot.odd, spot.odd_row
    above = jnp.where(spot.has_above, jnp.where(odd_row, first[...], second[...]), 0.0)
    below = jnp.where(spot.has_below, jnp.where(odd_row, second[...], first[...]), 0.0)
    for part in range(2):
        tall[part, :RIM] = above[part * RIM : (part + 1) * RIM]
        tall[part, RIM : RIM + side] = tile[part]
        tall[part, RIM + side :] = below[part * RIM : (part + 1) * RIM]
    low, high = pack(tall[0], tall[1])
    rows = low.shape[0]
    near[:rows] = jnp.where(odd, low, high)
    near[rows : rows + TILE] = above[2 * RIM :]
    near[rows + TILE : rows + 2 * TILE] = meta[...]
    near[rows + 2 * TILE :] = below[2 * RIM :]
    out = jnp.where(odd, high, low)
    far[:RIM] = jnp.where(odd_row, out[RIM + side :], out[:RIM])
    far[RIM:] = jnp.where(odd_row, below[2 * RIM :], above[2 * RIM :])


def window_place(starts, step, slot, width):
    row = starts[3 * step, slot] + RIM
    col = starts[3 * step + 1, slot]
    base = pl.multiple_of(row // TILE * TILE, TILE)
    lane = lanes((width + TILE, width))
    outside = (lane < col) | (lane >= width + col)
    return pl.ds(base, width + TILE), row - base, col, outside


def take_windows(starts, field, wins, weight, step):
    slots, _, width, _ = wins.shape
    tiles = width // TILE
    sub = lax.broadcasted_iota(jnp.int32, (tiles, TILE, width), 1)
    total = None
    for slot in range(slots):
        rows, skew, col, outside = window_place(starts, step, slot, width)
        live = jnp.where(slot < starts[3 * step + 2, 0], 1.0, 0.0).astype(jnp.float32)
        lift = jnp.where(skew > 0, TILE - skew, 0)
        back = lane_turn(-col, width)
        power = None
        for part in range(2):
            mixed = jnp.where(outside, field[part, rows, width:], field[part, rows, :width])
            turned = pltpu.roll(mixed.reshape(tiles + 1, TILE, width), lift, 1)
            lined = jnp.where(sub < TILE - skew, turned[:-1], turned[1:])
            win = pltpu.roll(lined.reshape(width, width), back, 1)
            wins[slot, part] = win
            power = win * win if power is None else power + win * win
        total = power * live if total is None else total + power * live
    weight[...] = total


def field_kernel(scan, tall, near, far, wins, weight, field, *, step):
    spot = Spot()
    width = tall.shape[2]
    rows = tall.shape[1]
    from_near, from_far = near[:rows], jnp.where(spot.has_far, far[:rows], 0.0)
    sides = unpack(
        jnp.where(spot.odd, from_far, from_near), jnp.where(spot.odd, from_near, from_far)
    )
    for part in range(2):
        field[part, :rows, :width] = tall[part]
        field[part, :rows, width:] = sides[part]
        field[part, rows:] = jnp.zeros_like(field[part, rows:])
    starts = Plain(scan[...])
    take_windows(starts, field, wins, weight, step)


def slots_kernel(
    scan, wins, win_weight, probe, amps, tables,
    core_out, far_out, keep_out, sums_out, sums, totals, psis, *, step,
):
    starts = Plain(scan[...])
    spot = Spot()
    width = probe.shape[1]
    rows_all = sums_out.shape[1]
    slots = amps.shape[0]
    odd = spot.odd
    sums[...] = jnp.zeros_like(sums)
    cos_h, cos_l, sin_h, sin_l, neg_h, neg_l = (tables[k] for k in range(6))

    def square(left_up, right_up, left_down, right_down):
        upper = jnp.concatenate([left_up, right_up], 1)
        return jnp.concatenate([upper, jnp.concatenate([left_down, right_down], 1)], 0)

    full_h, full_l = square(cos_h, neg_h, sin_h, cos_h), square(cos_l, neg_l, sin_l, cos_l)
    flip_h, flip_l = square(cos_h, sin_h, neg_h, cos_h), square(cos_l, sin_l, neg_l, cos_l)
    pro_r, pro_i = probe[0], probe[1]
    columns = []
    for slot in range(slots):
        psi_r = pro_r * wins[slot, 0] - pro_i * wins[slot, 1]
        psi_i = pro_r * wins[slot, 1] + pro_i * wins[slot, 0]
        psis[slot, 0] = psi_r
        psis[slot, 1] = psi_i
        columns.append(jnp.concatenate([psi_r, psi_i], 0))

    def block(value, k):
        return value[k * width : (k + 1) * width]

    def turn(half):
        parts = []
        for k in range(slots):
            both = half[:, k * width : (k + 1) * width]
            parts.append(jnp.concatenate([both[:width], both[width:]], 1))
        return jnp.concatenate(parts, 0)

    half = left_product(full_h, full_l, jnp.concatenate(columns, 1))
    wave = right_product(turn(half), flip_h, flip_l)
    columns = []
    for slot in range(slots):
        far_r, far_i = block(wave, slot)[:, :width], block(wave, slot)[:, width:]
        factor = amps[slot] * lax.rsqrt(jnp.maximum(far_r * far_r + far_i * far_i, 1.0))
        columns.append(jnp.concatenate([far_r * factor, far_i * factor], 0))
    half = left_product(flip_h, flip_l, jnp.concatenate(columns, 1))
    wave = right_product(turn(half), full_h, full_l)
    total = None
    for slot in range(slots):
        rows, skew, col, outside = window_place(starts, step, slot, width)
        ahead = lane_turn(col, width)
        live = jnp.where(slot < starts[3 * step + 2, 0], 1.0, 0.0).astype(jnp.float32)
        win_r, win_i = wins[slot, 0], wins[slot, 1]
        chi_r = (block(wave, slot)[:, :width] - psis[slot, 0]) * live
        chi_i = (block(wave, slot)[:, width:] - psis[slot, 1]) * live

        def deposit(part, term):
            grown = grow_rows(pltpu.roll(term, ahead, 1), skew)
            sums[part, rows, :width] += jnp.where(outside, 0.0, grown)
            sums[part, rows, width:] += jnp.where(outside, grown, 0.0)

        deposit(0, pro_r * chi_r + pro_i * chi_i)
        deposit(1, pro_r * chi_i - pro_i * chi_r)
        terms = (win_r * chi_r + win_i * chi_i, win_r * chi_i - win_i * chi_r)
        total = terms if total is None else tuple(a + b for a, b in zip(total, terms))
    half = width // 2
    totals[0], totals[1], totals[2] = total[0], total[1], win_weight[...]
    kept = pl.ds(pl.multiple_of(spot.side * half, half), half)
    given = pl.ds(pl.multiple_of((1 - spot.side) * half, half), half)
    for part in range(3):
        keep_out[part * half : (part + 1) * half] = totals[part, kept]
        core_out[part * half : (part + 1) * half] = totals[part, given]
    for part in range(2):
        sums_out[part] = sums[part, :rows_all, :width]
    low, high = pack(sums[0, :rows_all, width:], sums[1, :rows_all, width:])
    core_out[3 * half :] = jnp.where(odd, high, low)
    far_out[...] = jnp.where(odd, low, high)


def folded(spot, tall, near, far):
    start = near.shape[0] - tall.shape[1]
    odd = spot.odd
    from_near, from_far = near[start:], jnp.where(spot.has_far, far[...], 0.0)
    extra = unpack(jnp.where(odd, from_near, from_far), jnp.where(odd, from_far, from_near))
    return tall[0] + extra[0], tall[1] + extra[1]


def fold_kernel(tall, near, far, first, second):
    rows = first.shape[1]
    spot = Spot()
    odd_row = spot.odd_row
    whole = folded(spot, tall, near, far)
    for part in range(2):
        up, down = whole[part][:rows], whole[part][rows:]
        first[part] = jnp.where(odd_row, up, down)
        second[part] = jnp.where(odd_row, down, up)


def last_fold_kernel(tall, near, far, middle, first, second):
    rows = middle.shape[1]
    spot = Spot()
    odd_row = spot.odd_row
    whole = folded(spot, tall, near, far)
    for part in range(2):
        up, down = whole[part][:RIM], whole[part][RIM + rows :]
        middle[part] = whole[part][RIM : RIM + rows]
        first[part] = jnp.where(odd_row, up, down)
        second[part] = jnp.where(odd_row, down, up)


def weight_kernel(metas, probe, out, spread, *, step, slots):
    width = probe.shape[1]
    lane = lanes((width + TILE, width))
    spread[...] = jnp.zeros_like(spread)
    weight = probe[0] * probe[0] + probe[1] * probe[1]
    for index in range(metas.shape[0]):
        count = metas[index, (3 * step + 2) * slots]
        for slot in range(slots):
            row = metas[index, 3 * step * slots + slot] + (RIM + width + (index // 3 - 1) * width)
            col = metas[index, (3 * step + 1) * slots + slot] + (index % 3 - 1) * width

            base = pl.multiple_of(row // TILE * TILE, TILE)
            grown = grow_rows(pltpu.roll(weight, lax.rem(col + 2 * width, width), 1), row - base)
            edge = jnp.where(slot < count, col, 2 * width)
            inside = (lane >= edge) & (lane < width + edge)
            spread[pl.ds(base, width + TILE)] += jnp.where(inside, grown, 0.0)

    out[...] = spread[width : width + out.shape[0]]


def update_kernel(tall, sent_1, sent_2, got_1, got_2, weight, _, new_tall, near, far):
    rows = sent_1.shape[1]
    spot = Spot()
    odd, odd_row = spot.odd, spot.odd_row
    for part in range(2):
        up = jnp.where(odd_row, sent_1[part], sent_2[part])
        down = jnp.where(odd_row, sent_2[part], sent_1[part])
        above = jnp.where(odd_row, got_1[part], got_2[part])
        below = jnp.where(odd_row, got_2[part], got_1[part])
        up = up + jnp.where(spot.has_above, above, 0.0)
        down = down + jnp.where(spot.has_below, below, 0.0)
        head = tall[part, :rows] + up / (weight[:rows] + EPS)
        tail = tall[part, rows:] + down / (weight[rows:] + EPS)
        new_tall[part, :RIM] = jnp.where(spot.has_above, head[:RIM], 0.0)
        new_tall[part, RIM:rows] = head[RIM:]
        new_tall[part, rows : 2 * rows - RIM] = tail[: rows - RIM]
        new_tall[part, 2 * rows - RIM :] = jnp.where(spot.has_below, tail[rows - RIM :], 0.0)
    low, high = pack(new_tall[0], new_tall[1])
    near[...] = jnp.where(odd, low, high)
    far[...] = jnp.where(odd, high, low)


def last_kernel(tall, middle, got_1, got_2, weight, mine, other, tile, probe):
    side = tile.shape[1]
    half = mine.shape[1]
    spot = Spot()
    odd, odd_row = spot.odd, spot.odd_row
    for part in range(2):
        above = jnp.where(odd_row, got_1[part], got_2[part])
        below = jnp.where(odd_row, got_2[part], got_1[part])
        above = jnp.where(spot.has_above, above, 0.0)
        below = jnp.where(spot.has_below, below, 0.0)
        num = middle[part] + jnp.concatenate([above, below], 0)
        tile[part] = tall[part, RIM : RIM + side] + num / (weight[RIM : RIM + side] + EPS)
        probe[part, :half] = jnp.where(odd, other[part], mine[part])
        probe[part, half:] = jnp.where(odd, mine[part], other[part])


def call(kernel, shapes, places, operands, flops=1000000, moved=MIB, scratch=(), more=(), limit=16):
    vmem = pl.BlockSpec(memory_space=pltpu.VMEM)
    smem = pl.BlockSpec(memory_space=pltpu.SMEM)
    anywhere = pl.BlockSpec(memory_space=pl.ANY)
    return pl.pallas_call(
        kernel,
        out_shape=tuple(jax.ShapeDtypeStruct(shape, jnp.float32) for shape in shapes),
        in_specs=[{"s": smem, "a": anywhere}.get(where, vmem) for where in places.ljust(len(operands), "v")],
        out_specs=tuple(vmem for _ in shapes),
        scratch_shapes=[pltpu.VMEM(shape, jnp.float32) for shape in scratch] + list(more),
        compiler_params=pltpu.CompilerParams(vmem_limit_bytes=limit * MIB),
        cost_estimate=pl.CostEstimate(flops=flops, bytes_accessed=moved, transcendentals=0),
    )(*operands)


def swap(value, axis, bit):
    return lax.ppermute(value, axis, [(i, i ^ bit) for i in range(lax.axis_size(axis))])


def swap_far(value):
    rows, cols = lax.axis_size("row"), lax.axis_size("col")
    pairs = []
    for row in range(rows):
        for col in range(cols):
            to_row, to_col = row, col + (1 if col % 2 else -1)
            if not 0 <= to_col < cols:
                to_row, to_col = row ^ 1, col
            pairs.append((row * cols + col, to_row * cols + to_col))
    return lax.ppermute(value, AXES, pairs)


def swap_rows(value):
    rows, cols = lax.axis_size("row"), lax.axis_size("col")
    pairs = []
    for row in range(rows):
        for col in range(cols):
            to_row, to_col = row + (1 if row % 2 else -1), col
            if not 0 <= to_row < rows:
                to_row, to_col = row, col ^ 1
            pairs.append((row * cols + col, to_row * cols + to_col))
    return lax.ppermute(value, AXES, pairs)


def after(*values):
    return lax.optimization_barrier(values)


def chip_steps():
    steps = [("row", 1)]
    for axis in ("col", "row"):
        bit = 2
        while bit < lax.axis_size(axis):
            steps.append((axis, bit))
            bit *= 2
    return steps


def swap_both(value):
    rows, cols = lax.axis_size("row"), lax.axis_size("col")
    pairs = [(r * cols + c, (r ^ 1) * cols + (c ^ 2)) for r in range(rows) for c in range(cols)]
    return lax.ppermute(value, AXES, pairs)


def chain_steps():
    return lax.axis_size("row").bit_length() - 2


def add_plane(part, weight):
    part_y, part_x, part_xy = swap(part, "row", 1), swap(part, "col", 2), swap_both(part)
    if weight is not None:
        part_xy, weight = after(part_xy, weight)
    return (part + part_y) + (part_x + part_xy)


def add_step(part, step):
    return part + swap(part, *step)


def body(object_field, probe, positions, counts, amplitude):
    side = object_field.shape[1]
    width = probe.shape[1]
    half = width // 2
    steps = positions.shape[2]
    slots = positions.shape[3]
    tall_rows = side + 2 * RIM
    row, col = lax.axis_index("row"), lax.axis_index("col")
    odd, odd_row = col % 2, row % 2
    outer = (col == 0) | (col == lax.axis_size("col") - 1)
    tables = jnp.asarray(dft_tables(width))

    offsets = jnp.swapaxes(positions[0, 0], 1, 2)
    flat = 2 * RIM
    first, second, meta = call(
        first_kernel,
        ((flat + TILE, width), (flat + TILE, width), (TILE, width)),
        "aaa",
        (object_field, offsets, counts[0]),
        more=(
            pltpu.VMEM(offsets.shape, jnp.int32),
            pltpu.VMEM((1, steps), jnp.int32),
            pltpu.SemaphoreType.DMA((6,)),
        ),
        limit=60,
    )
    scan = meta[: 3 * steps, :slots].astype(jnp.int32)
    first, second = swap(first, "row", 1), swap_rows(second)
    (early,) = call(
        early_kernel,
        ((RIM + side + 2 * TILE, width),),
        "",
        (object_field, meta, first),
    )
    early = swap_far(early)
    tall, near, late = call(
        strips_kernel,
        ((2, tall_rows, side), (tall_rows + 3 * TILE, width), (RIM + TILE, width)),
        "",
        (object_field, meta, first, second),
    )
    near, late = swap(near, "col", 1), swap_far(late)
    turned = odd_row != 0
    sides = early[:RIM], late[:RIM]
    ends = early[RIM + side : RIM + side + TILE], late[RIM:]
    far = jnp.concatenate(
        [
            jnp.where(turned, sides[0], sides[1]),
            early[RIM : RIM + side],
            jnp.where(turned, sides[1], sides[0]),
            jnp.where(turned, ends[0], ends[1]),
            early[RIM + side + TILE :],
            jnp.where(turned, ends[1], ends[0]),
        ],
        0,
    )

    def three(value):
        return value[tall_rows:].reshape(3, TILE, width)[:, : 3 * steps, :slots]

    above = jnp.where(row > 0, jnp.where(odd_row != 0, first[flat:], second[flat:]), 0.0)
    below = jnp.where(row < lax.axis_size("row") - 1, jnp.where(odd_row != 0, second[flat:], first[flat:]), 0.0)
    here = jnp.stack([above, meta, below])[:, : 3 * steps, :slots]
    sides = three(near), jnp.where(outer, 0.0, three(far))
    left = jnp.where(odd != 0, sides[0], sides[1])
    right = jnp.where(odd != 0, sides[1], sides[0])
    metas = jnp.stack([left, here, right], 1).reshape(9, -1).astype(jnp.int32)

    def windows(step, tall, near, far):
        return call(
            functools.partial(field_kernel, step=step),
            ((slots, 2, width, width), (width, width)),
            "",
            (scan, tall, near, far),
            scratch=((2, tall_rows + TILE, 2 * width),),
        )

    wins, win_weight = windows(0, tall, near, far)
    current = probe
    for step in range(steps):
        last = step == steps - 1
        core, out_far, kept, sums = call(
            functools.partial(slots_kernel, step=step),
            (
                (3 * half + tall_rows, width),
                (tall_rows, width),
                (3 * half, width),
                (2, tall_rows, width),
            ),
            "",
            (scan, wins, win_weight, current, amplitude[0, 0, step], tables),
            flops=slots * 96 * width * width * width,
            moved=4 * MIB,
            scratch=(
                (2, tall_rows + TILE, 2 * width),
                (3, width, width),
                (slots, 2, width, width),
            ),
            limit=24,
        )
        core = swap(core, "col", 1)
        out_far = swap_far(out_far)
        (weight,) = call(
            functools.partial(weight_kernel, step=step, slots=slots),
            ((tall_rows, width),),
            "s",
            (metas, current),
            scratch=((tall_rows + 2 * width + TILE, width),),
        )
        part = kept + core[: 3 * half]
        if last:
            middle, sent_1, sent_2 = call(
                last_fold_kernel,
                ((2, side, width), (2, RIM, width), (2, RIM, width)),
                "",
                (sums, core, out_far),
                moved=16 * MIB,
            )
            got_1, got_2 = swap(sent_1, "row", 1), swap_rows(sent_2)
            part = add_plane(part, weight)
            for other_step in chip_steps()[-chain_steps() : -1]:
                part = add_step(part, other_step)
            part = add_step(part, chip_steps()[-1])
        else:
            sent_1, sent_2 = call(
                fold_kernel,
                ((2, tall_rows // 2, width), (2, tall_rows // 2, width)),
                "",
                (sums, core, out_far),
            )
            got_1, got_2 = swap(sent_1, "row", 1), swap_rows(sent_2)
            part = add_plane(part, weight)
            for other_step in chip_steps()[-chain_steps() : -1]:
                part = add_step(part, other_step)
            tall, near, far = call(
                update_kernel,
                ((2, tall_rows, side), (tall_rows, width), (tall_rows, width)),
                "",
                (tall, sent_1, sent_2, got_1, got_2, weight, part[:TILE]),
            )
            near = swap(near, "col", 1)
            far_1, far_2 = swap_far(far[: tall_rows // 2]), swap_far(far[tall_rows // 2 :])
            part = add_step(part, chip_steps()[-1])
            far = jnp.concatenate([far_1, far_2], 0)
            wins, win_weight = windows(step + 1, tall, near, far)
        mine = lax.dynamic_slice_in_dim(current, odd * half, half, 1)
        part = part.reshape(3, half, width)
        mine = mine + part[:2] / (part[2] + EPS)[None]
        other = swap(mine, "col", 1)
        if last:
            return call(
                last_kernel,
                ((2, side, side), (2, width, width)),
                "",
                (tall, middle, got_1, got_2, weight, mine, other),
                moved=4 * MIB,
            )
        low = jnp.where(odd == 0, mine, other)
        high = jnp.where(odd == 0, other, mine)
        current = jnp.concatenate([low, high], 1)


def solution(mesh):
    return jax.shard_map(
        body,
        mesh=mesh,
        in_specs=(
            P(None, "row", "col"),
            P(),
            P("row", "col", None, None, None),
            P("row", "col", None),
            P("row", "col", None, None, None, None),
        ),
        out_specs=(P(None, "row", "col"), P()),
        check_vma=False,
    )
```

```python
import functools
import math

import jax
import jax.numpy as jnp
import numpy as np
from jax import lax
from jax.experimental import pallas as pl
from jax.experimental.pallas import tpu as pltpu
from jax.sharding import PartitionSpec as P

RIM = 64
TILE = 8
EPS = 0.1
AXES = ("row", "col")
MIB = 1024 * 1024


def dft_tables(size):
    index = np.arange(size)
    angle = (index[:, None] * index[None, :] % size) * (-2.0 * math.pi / size)
    cosine = np.cos(angle) / math.sqrt(size)
    sine = np.sin(angle) / math.sqrt(size)
    tables = []
    for table in (cosine.astype(np.float32), sine.astype(np.float32)):
        high = table.astype(jnp.bfloat16)
        low = (table - high.astype(np.float32)).astype(jnp.bfloat16)
        tables += [high, low]
    return np.stack(tables + [-tables[2], -tables[3]])


def split(value):
    high = value.astype(jnp.bfloat16)
    return high, (value - high.astype(jnp.float32)).astype(jnp.bfloat16)


def mul(left, right):
    return jnp.dot(left, right, preferred_element_type=jnp.float32)


def left_product(high, low, value):
    first, second = split(value)
    return mul(high, first) + (mul(high, second) + mul(low, first))


def right_product(value, high, low):
    first, second = split(value)
    return mul(first, high) + (mul(second, high) + mul(first, low))


def lanes(shape):
    return lax.broadcasted_iota(jnp.int32, shape, 1)


def pack(real, imag):
    half = real.shape[1] // 2
    first = lanes(real.shape) < half
    low = jnp.where(first, real, pltpu.roll(imag, half, 1))
    high = jnp.where(first, pltpu.roll(real, half, 1), imag)
    return low, high


def unpack(low, high):
    half = low.shape[1] // 2
    first = lanes(low.shape) < half
    real = jnp.where(first, low, pltpu.roll(high, half, 1))
    imag = jnp.where(first, pltpu.roll(low, half, 1), high)
    return real, imag


def grow_rows(term, skew):
    count, width = term.shape
    tiles = count // TILE
    sub = lax.broadcasted_iota(jnp.int32, (tiles, TILE, width), 1)
    turned = pltpu.roll(term.reshape(tiles, TILE, width), skew, 1)
    late = jnp.where(sub < skew, turned, 0.0)
    soon = jnp.where(sub < skew, 0.0, turned)
    blank = jnp.zeros((1, TILE, width), jnp.float32)
    grown = jnp.concatenate([soon, blank], 0) + jnp.concatenate([blank, late], 0)
    return grown.reshape(count + TILE, width)


def lane_turn(col, width):
    return jnp.where(col < 0, col + width, col)


class Plain:
    def __init__(self, value):
        self.value = value

    def __getitem__(self, where):
        row, col = where
        return self.value[row, col]


class Spot:
    def __init__(self):
        row, col = lax.axis_index("row"), lax.axis_index("col")
        self.side = lax.rem(col, 2)
        self.odd = self.side != 0
        self.row_side = lax.rem(row, 2)
        self.odd_row = self.row_side != 0
        self.has_above = row != 0
        self.has_below = row != lax.axis_size("row") - 1
        self.has_far = (col != 0) & (col != lax.axis_size("col") - 1)


def first_kernel(tile, offsets, counts, first, second, meta, offsets_here, counts_here, sems):
    spot = Spot()
    side = tile.shape[1]
    steps, _, slots = offsets.shape
    near_edge = pl.multiple_of(spot.row_side * RIM, RIM)
    copies = [
        pltpu.make_async_copy(offsets, offsets_here, sems.at[0]),
        pltpu.make_async_copy(counts, counts_here, sems.at[1]),
    ]
    for part in range(2):
        rows = pl.ds(part * RIM, RIM)
        lower = pl.ds(side - RIM - near_edge, RIM)
        upper = pl.ds(near_edge, RIM)
        copies.append(pltpu.make_async_copy(tile.at[part, lower], first.at[rows], sems.at[2 + part]))
        copies.append(pltpu.make_async_copy(tile.at[part, upper], second.at[rows], sems.at[4 + part]))
    for copy in copies:
        copy.start()
    meta[...] = jnp.zeros_like(meta)
    for copy in copies[:2]:
        copy.wait()
    for step in range(steps):
        meta[3 * step : 3 * step + 2, :slots] = offsets_here[step].astype(jnp.float32)
        count = counts_here[:, step : step + 1].astype(jnp.float32)
        meta[3 * step + 2 : 3 * step + 3] = jnp.broadcast_to(count, (1, meta.shape[1]))
    first[2 * RIM :] = meta[...]
    second[2 * RIM :] = meta[...]
    for copy in copies[2:]:
        copy.wait()


def early_kernel(tile, meta, first, far):
    odd = Spot().odd
    side = tile.shape[1]
    for at, real, imag in ((0, first[:RIM], first[RIM : 2 * RIM]), (RIM, tile[0], tile[1])):
        low, high = pack(real, imag)
        far[at : at + low.shape[0]] = jnp.where(odd, high, low)
    far[RIM + side : RIM + side + TILE] = first[2 * RIM :]
    far[RIM + side + TILE :] = meta[...]


def strips_kernel(tile, meta, first, second, tall, near, far):
    side = tile.shape[1]
    spot = Spot()
    odd, odd_row = spot.odd, spot.odd_row
    above = jnp.where(spot.has_above, jnp.where(odd_row, first[...], second[...]), 0.0)
    below = jnp.where(spot.has_below, jnp.where(odd_row, second[...], first[...]), 0.0)
    for part in range(2):
        tall[part, :RIM] = above[part * RIM : (part + 1) * RIM]
        tall[part, RIM : RIM + side] = tile[part]
        tall[part, RIM + side :] = below[part * RIM : (part + 1) * RIM]
    low, high = pack(tall[0], tall[1])
    rows = low.shape[0]
    near[:rows] = jnp.where(odd, low, high)
    near[rows : rows + TILE] = above[2 * RIM :]
    near[rows + TILE : rows + 2 * TILE] = meta[...]
    near[rows + 2 * TILE :] = below[2 * RIM :]
    out = jnp.where(odd, high, low)
    far[:RIM] = jnp.where(odd_row, out[RIM + side :], out[:RIM])
    far[RIM:] = jnp.where(odd_row, below[2 * RIM :], above[2 * RIM :])


def window_place(starts, step, slot, width):
    row = starts[3 * step, slot] + RIM
    col = starts[3 * step + 1, slot]
    base = pl.multiple_of(row // TILE * TILE, TILE)
    lane = lanes((width + TILE, width))
    outside = (lane < col) | (lane >= width + col)
    return pl.ds(base, width + TILE), row - base, col, outside


def take_windows(starts, field, wins, weight, step):
    slots, _, width, _ = wins.shape
    tiles = width // TILE
    sub = lax.broadcasted_iota(jnp.int32, (tiles, TILE, width), 1)
    total = None
    for slot in range(slots):
        rows, skew, col, outside = window_place(starts, step, slot, width)
        live = jnp.where(slot < starts[3 * step + 2, 0], 1.0, 0.0).astype(jnp.float32)
        lift = jnp.where(skew > 0, TILE - skew, 0)
        back = lane_turn(-col, width)
        power = None
        for part in range(2):
            mixed = jnp.where(outside, field[part, rows, width:], field[part, rows, :width])
            turned = pltpu.roll(mixed.reshape(tiles + 1, TILE, width), lift, 1)
            lined = jnp.where(sub < TILE - skew, turned[:-1], turned[1:])
            win = pltpu.roll(lined.reshape(width, width), back, 1)
            wins[slot, part] = win
            power = win * win if power is None else power + win * win
        total = power * live if total is None else total + power * live
    weight[...] = total


def field_kernel(scan, tall, near, far, wins, weight, field, *, step):
    spot = Spot()
    width = tall.shape[2]
    rows = tall.shape[1]
    from_near, from_far = near[:rows], jnp.where(spot.has_far, far[:rows], 0.0)
    sides = unpack(
        jnp.where(spot.odd, from_far, from_near), jnp.where(spot.odd, from_near, from_far)
    )
    for part in range(2):
        field[part, :rows, :width] = tall[part]
        field[part, :rows, width:] = sides[part]
        field[part, rows:] = jnp.zeros_like(field[part, rows:])
    starts = Plain(scan[...])
    take_windows(starts, field, wins, weight, step)


def slots_kernel(
    scan, wins, win_weight, probe, amps, tables,
    core_out, far_out, keep_out, sums_out, sums, totals, psis, *, step,
):
    starts = Plain(scan[...])
    spot = Spot()
    width = probe.shape[1]
    rows_all = sums_out.shape[1]
    slots = amps.shape[0]
    odd = spot.odd
    sums[...] = jnp.zeros_like(sums)
    cos_h, cos_l, sin_h, sin_l, neg_h, neg_l = (tables[k] for k in range(6))

    def square(left_up, right_up, left_down, right_down):
        upper = jnp.concatenate([left_up, right_up], 1)
        return jnp.concatenate([upper, jnp.concatenate([left_down, right_down], 1)], 0)

    full_h, full_l = square(cos_h, neg_h, sin_h, cos_h), square(cos_l, neg_l, sin_l, cos_l)
    flip_h, flip_l = square(cos_h, sin_h, neg_h, cos_h), square(cos_l, sin_l, neg_l, cos_l)
    pro_r, pro_i = probe[0], probe[1]
    columns = []
    for slot in range(slots):
        psi_r = pro_r * wins[slot, 0] - pro_i * wins[slot, 1]
        psi_i = pro_r * wins[slot, 1] + pro_i * wins[slot, 0]
        psis[slot, 0] = psi_r
        psis[slot, 1] = psi_i
        columns.append(jnp.concatenate([psi_r, psi_i], 0))

    def block(value, k):
        return value[k * width : (k + 1) * width]

    def turn(half):
        parts = []
        for k in range(slots):
            both = half[:, k * width : (k + 1) * width]
            parts.append(jnp.concatenate([both[:width], both[width:]], 1))
        return jnp.concatenate(parts, 0)

    half = left_product(full_h, full_l, jnp.concatenate(columns, 1))
    wave = right_product(turn(half), flip_h, flip_l)
    columns = []
    for slot in range(slots):
        far_r, far_i = block(wave, slot)[:, :width], block(wave, slot)[:, width:]
        factor = amps[slot] * lax.rsqrt(jnp.maximum(far_r * far_r + far_i * far_i, 1.0))
        columns.append(jnp.concatenate([far_r * factor, far_i * factor], 0))
    half = left_product(flip_h, flip_l, jnp.concatenate(columns, 1))
    wave = right_product(turn(half), full_h, full_l)
    total = None
    for slot in range(slots):
        rows, skew, col, outside = window_place(starts, step, slot, width)
        ahead = lane_turn(col, width)
        live = jnp.where(slot < starts[3 * step + 2, 0], 1.0, 0.0).astype(jnp.float32)
        win_r, win_i = wins[slot, 0], wins[slot, 1]
        chi_r = (block(wave, slot)[:, :width] - psis[slot, 0]) * live
        chi_i = (block(wave, slot)[:, width:] - psis[slot, 1]) * live

        def deposit(part, term):
            grown = grow_rows(pltpu.roll(term, ahead, 1), skew)
            sums[part, rows, :width] += jnp.where(outside, 0.0, grown)
            sums[part, rows, width:] += jnp.where(outside, grown, 0.0)

        deposit(0, pro_r * chi_r + pro_i * chi_i)
        deposit(1, pro_r * chi_i - pro_i * chi_r)
        terms = (win_r * chi_r + win_i * chi_i, win_r * chi_i - win_i * chi_r)
        total = terms if total is None else tuple(a + b for a, b in zip(total, terms))
    half = width // 2
    totals[0], totals[1], totals[2] = total[0], total[1], win_weight[...]
    kept = pl.ds(pl.multiple_of(spot.side * half, half), half)
    given = pl.ds(pl.multiple_of((1 - spot.side) * half, half), half)
    for part in range(3):
        keep_out[part * half : (part + 1) * half] = totals[part, kept]
        core_out[part * half : (part + 1) * half] = totals[part, given]
    for part in range(2):
        sums_out[part] = sums[part, :rows_all, :width]
    low, high = pack(sums[0, :rows_all, width:], sums[1, :rows_all, width:])
    core_out[3 * half :] = jnp.where(odd, high, low)
    far_out[...] = jnp.where(odd, low, high)


def folded(spot, tall, near, far):
    start = near.shape[0] - tall.shape[1]
    odd = spot.odd
    from_near, from_far = near[start:], jnp.where(spot.has_far, far[...], 0.0)
    extra = unpack(jnp.where(odd, from_near, from_far), jnp.where(odd, from_far, from_near))
    return tall[0] + extra[0], tall[1] + extra[1]


def fold_kernel(tall, near, far, first, second):
    rows = first.shape[1]
    spot = Spot()
    odd_row = spot.odd_row
    whole = folded(spot, tall, near, far)
    for part in range(2):
        up, down = whole[part][:rows], whole[part][rows:]
        first[part] = jnp.where(odd_row, up, down)
        second[part] = jnp.where(odd_row, down, up)


def last_fold_kernel(tall, near, far, middle, first, second):
    rows = middle.shape[1]
    spot = Spot()
    odd_row = spot.odd_row
    whole = folded(spot, tall, near, far)
    for part in range(2):
        up, down = whole[part][:RIM], whole[part][RIM + rows :]
        middle[part] = whole[part][RIM : RIM + rows]
        first[part] = jnp.where(odd_row, up, down)
        second[part] = jnp.where(odd_row, down, up)


def weight_kernel(metas, probe, out, spread, *, step, slots):
    width = probe.shape[1]
    lane = lanes((width + TILE, width))
    spread[...] = jnp.zeros_like(spread)
    weight = probe[0] * probe[0] + probe[1] * probe[1]
    for index in range(metas.shape[0]):
        count = metas[index, (3 * step + 2) * slots]
        for slot in range(slots):
            row = metas[index, 3 * step * slots + slot] + (RIM + width + (index // 3 - 1) * width)
            col = metas[index, (3 * step + 1) * slots + slot] + (index % 3 - 1) * width

            base = pl.multiple_of(row // TILE * TILE, TILE)
            grown = grow_rows(pltpu.roll(weight, lax.rem(col + 2 * width, width), 1), row - base)
            edge = jnp.where(slot < count, col, 2 * width)
            inside = (lane >= edge) & (lane < width + edge)
            spread[pl.ds(base, width + TILE)] += jnp.where(inside, grown, 0.0)

    out[...] = spread[width : width + out.shape[0]]


def update_kernel(tall, sent_1, sent_2, got_1, got_2, weight, _, new_tall, near, far):
    rows = sent_1.shape[1]
    spot = Spot()
    odd, odd_row = spot.odd, spot.odd_row
    for part in range(2):
        up = jnp.where(odd_row, sent_1[part], sent_2[part])
        down = jnp.where(odd_row, sent_2[part], sent_1[part])
        above = jnp.where(odd_row, got_1[part], got_2[part])
        below = jnp.where(odd_row, got_2[part], got_1[part])
        up = up + jnp.where(spot.has_above, above, 0.0)
        down = down + jnp.where(spot.has_below, below, 0.0)
        head = tall[part, :rows] + up / (weight[:rows] + EPS)
        tail = tall[part, rows:] + down / (weight[rows:] + EPS)
        new_tall[part, :RIM] = jnp.where(spot.has_above, head[:RIM], 0.0)
        new_tall[part, RIM:rows] = head[RIM:]
        new_tall[part, rows : 2 * rows - RIM] = tail[: rows - RIM]
        new_tall[part, 2 * rows - RIM :] = jnp.where(spot.has_below, tail[rows - RIM :], 0.0)
    low, high = pack(new_tall[0], new_tall[1])
    near[...] = jnp.where(odd, low, high)
    far[...] = jnp.where(odd, high, low)


def last_kernel(tall, middle, got_1, got_2, weight, mine, other, tile, probe):
    side = tile.shape[1]
    half = mine.shape[1]
    spot = Spot()
    odd, odd_row = spot.odd, spot.odd_row
    for part in range(2):
        above = jnp.where(odd_row, got_1[part], got_2[part])
        below = jnp.where(odd_row, got_2[part], got_1[part])
        above = jnp.where(spot.has_above, above, 0.0)
        below = jnp.where(spot.has_below, below, 0.0)
        num = middle[part] + jnp.concatenate([above, below], 0)
        tile[part] = tall[part, RIM : RIM + side] + num / (weight[RIM : RIM + side] + EPS)
        probe[part, :half] = jnp.where(odd, other[part], mine[part])
        probe[part, half:] = jnp.where(odd, mine[part], other[part])


def call(kernel, shapes, places, operands, flops=1000000, moved=MIB, scratch=(), more=(), limit=16):
    vmem = pl.BlockSpec(memory_space=pltpu.VMEM)
    smem = pl.BlockSpec(memory_space=pltpu.SMEM)
    anywhere = pl.BlockSpec(memory_space=pl.ANY)
    return pl.pallas_call(
        kernel,
        out_shape=tuple(jax.ShapeDtypeStruct(shape, jnp.float32) for shape in shapes),
        in_specs=[{"s": smem, "a": anywhere}.get(where, vmem) for where in places.ljust(len(operands), "v")],
        out_specs=tuple(vmem for _ in shapes),
        scratch_shapes=[pltpu.VMEM(shape, jnp.float32) for shape in scratch] + list(more),
        compiler_params=pltpu.CompilerParams(vmem_limit_bytes=limit * MIB),
        cost_estimate=pl.CostEstimate(flops=flops, bytes_accessed=moved, transcendentals=0),
    )(*operands)


def swap(value, axis, bit):
    return lax.ppermute(value, axis, [(i, i ^ bit) for i in range(lax.axis_size(axis))])


def swap_far(value):
    rows, cols = lax.axis_size("row"), lax.axis_size("col")
    pairs = []
    for row in range(rows):
        for col in range(cols):
            to_row, to_col = row, col + (1 if col % 2 else -1)
            if not 0 <= to_col < cols:
                to_row, to_col = row ^ 1, col
            pairs.append((row * cols + col, to_row * cols + to_col))
    return lax.ppermute(value, AXES, pairs)


def swap_rows(value):
    rows, cols = lax.axis_size("row"), lax.axis_size("col")
    pairs = []
    for row in range(rows):
        for col in range(cols):
            to_row, to_col = row + (1 if row % 2 else -1), col
            if not 0 <= to_row < rows:
                to_row, to_col = row, col ^ 1
            pairs.append((row * cols + col, to_row * cols + to_col))
    return lax.ppermute(value, AXES, pairs)


def after(*values):
    return lax.optimization_barrier(values)


def chip_steps():
    steps = [("row", 1)]
    for axis in ("col", "row"):
        bit = 2
        while bit < lax.axis_size(axis):
            steps.append((axis, bit))
            bit *= 2
    return steps


def swap_both(value):
    rows, cols = lax.axis_size("row"), lax.axis_size("col")
    pairs = [(r * cols + c, (r ^ 1) * cols + (c ^ 2)) for r in range(rows) for c in range(cols)]
    return lax.ppermute(value, AXES, pairs)


def add_plane(part, weight):
    part_y, part_x, part_xy = swap(part, "row", 1), swap(part, "col", 2), swap_both(part)
    if weight is not None:
        part_xy, weight = after(part_xy, weight)
    return (part + part_y) + (part_x + part_xy)


def add_step(part, step):
    return part + swap(part, *step)


def body(object_field, probe, positions, counts, amplitude):
    side = object_field.shape[1]
    width = probe.shape[1]
    half = width // 2
    steps = positions.shape[2]
    slots = positions.shape[3]
    tall_rows = side + 2 * RIM
    row, col = lax.axis_index("row"), lax.axis_index("col")
    odd, odd_row = col % 2, row % 2
    outer = (col == 0) | (col == lax.axis_size("col") - 1)
    tables = jnp.asarray(dft_tables(width))

    offsets = jnp.swapaxes(positions[0, 0], 1, 2)
    flat = 2 * RIM
    first, second, meta = call(
        first_kernel,
        ((flat + TILE, width), (flat + TILE, width), (TILE, width)),
        "aaa",
        (object_field, offsets, counts[0]),
        more=(
            pltpu.VMEM(offsets.shape, jnp.int32),
            pltpu.VMEM((1, steps), jnp.int32),
            pltpu.SemaphoreType.DMA((6,)),
        ),
        limit=60,
    )
    scan = meta[: 3 * steps, :slots].astype(jnp.int32)
    first, second = swap(first, "row", 1), swap_rows(second)
    (early,) = call(
        early_kernel,
        ((RIM + side + 2 * TILE, width),),
        "",
        (object_field, meta, first),
    )
    early = swap_far(early)
    tall, near, late = call(
        strips_kernel,
        ((2, tall_rows, side), (tall_rows + 3 * TILE, width), (RIM + TILE, width)),
        "",
        (object_field, meta, first, second),
    )
    near, late = swap(near, "col", 1), swap_far(late)
    turned = odd_row != 0
    sides = early[:RIM], late[:RIM]
    ends = early[RIM + side : RIM + side + TILE], late[RIM:]
    far = jnp.concatenate(
        [
            jnp.where(turned, sides[0], sides[1]),
            early[RIM : RIM + side],
            jnp.where(turned, sides[1], sides[0]),
            jnp.where(turned, ends[0], ends[1]),
            early[RIM + side + TILE :],
            jnp.where(turned, ends[1], ends[0]),
        ],
        0,
    )

    def three(value):
        return value[tall_rows:].reshape(3, TILE, width)[:, : 3 * steps, :slots]

    above = jnp.where(row > 0, jnp.where(odd_row != 0, first[flat:], second[flat:]), 0.0)
    below = jnp.where(row < lax.axis_size("row") - 1, jnp.where(odd_row != 0, second[flat:], first[flat:]), 0.0)
    here = jnp.stack([above, meta, below])[:, : 3 * steps, :slots]
    sides = three(near), jnp.where(outer, 0.0, three(far))
    left = jnp.where(odd != 0, sides[0], sides[1])
    right = jnp.where(odd != 0, sides[1], sides[0])
    metas = jnp.stack([left, here, right], 1).reshape(9, -1).astype(jnp.int32)

    def windows(step, tall, near, far):
        return call(
            functools.partial(field_kernel, step=step),
            ((slots, 2, width, width), (width, width)),
            "",
            (scan, tall, near, far),
            scratch=((2, tall_rows + TILE, 2 * width),),
        )

    wins, win_weight = windows(0, tall, near, far)
    current = probe
    for step in range(steps):
        last = step == steps - 1
        core, out_far, kept, sums = call(
            functools.partial(slots_kernel, step=step),
            (
                (3 * half + tall_rows, width),
                (tall_rows, width),
                (3 * half, width),
                (2, tall_rows, width),
            ),
            "",
            (scan, wins, win_weight, current, amplitude[0, 0, step], tables),
            flops=slots * 96 * width * width * width,
            moved=4 * MIB,
            scratch=(
                (2, tall_rows + TILE, 2 * width),
                (3, width, width),
                (slots, 2, width, width),
            ),
            limit=24,
        )
        core = swap(core, "col", 1)
        out_far = swap_far(out_far)
        (weight,) = call(
            functools.partial(weight_kernel, step=step, slots=slots),
            ((tall_rows, width),),
            "s",
            (metas, current),
            scratch=((tall_rows + 2 * width + TILE, width),),
        )
        part = kept + core[: 3 * half]
        if last:
            middle, sent_1, sent_2 = call(
                last_fold_kernel,
                ((2, side, width), (2, RIM, width), (2, RIM, width)),
                "",
                (sums, core, out_far),
                moved=16 * MIB,
            )
            got_1, got_2 = swap(sent_1, "row", 1), swap_rows(sent_2)
            part = add_plane(part, weight)
            for other_step in chip_steps()[2:-1]:
                part = add_step(part, other_step)
            part = add_step(part, chip_steps()[-1])
        else:
            sent_1, sent_2 = call(
                fold_kernel,
                ((2, tall_rows // 2, width), (2, tall_rows // 2, width)),
                "",
                (sums, core, out_far),
            )
            got_1, got_2 = swap(sent_1, "row", 1), swap_rows(sent_2)
            part = add_plane(part, weight)
            for other_step in chip_steps()[2:-1]:
                part = add_step(part, other_step)
            tall, near, far = call(
                update_kernel,
                ((2, tall_rows, side), (tall_rows, width), (tall_rows, width)),
                "",
                (tall, sent_1, sent_2, got_1, got_2, weight, part[:TILE]),
            )
            near = swap(near, "col", 1)
            far_1, far_2 = swap_far(far[: tall_rows // 2]), swap_far(far[tall_rows // 2 :])
            part = add_step(part, chip_steps()[-1])
            far = jnp.concatenate([far_1, far_2], 0)
            wins, win_weight = windows(step + 1, tall, near, far)
        mine = lax.dynamic_slice_in_dim(current, odd * half, half, 1)
        part = part.reshape(3, half, width)
        mine = mine + part[:2] / (part[2] + EPS)[None]
        other = swap(mine, "col", 1)
        if last:
            return call(
                last_kernel,
                ((2, side, side), (2, width, width)),
                "",
                (tall, middle, got_1, got_2, weight, mine, other),
                moved=4 * MIB,
            )
        low = jnp.where(odd == 0, mine, other)
        high = jnp.where(odd == 0, other, mine)
        current = jnp.concatenate([low, high], 1)


def solution(mesh):
    return jax.shard_map(
        body,
        mesh=mesh,
        in_specs=(
            P(None, "row", "col"),
            P(),
            P("row", "col", None, None, None),
            P("row", "col", None),
            P("row", "col", None, None, None, None),
        ),
        out_specs=(P(None, "row", "col"), P()),
        check_vma=False,
    )
```

```python
import functools
import math

import jax
import jax.numpy as jnp
import numpy as np
from jax import lax
from jax.experimental import pallas as pl
from jax.experimental.pallas import tpu as pltpu
from jax.sharding import PartitionSpec as P

RIM = 64
TILE = 8
EPS = 0.1
AXES = ("row", "col")
MIB = 1024 * 1024


def dft_tables(size):
    index = np.arange(size)
    angle = (index[:, None] * index[None, :] % size) * (-2.0 * math.pi / size)
    cosine = np.cos(angle) / math.sqrt(size)
    sine = np.sin(angle) / math.sqrt(size)
    tables = []
    for table in (cosine.astype(np.float32), sine.astype(np.float32)):
        high = table.astype(jnp.bfloat16)
        low = (table - high.astype(np.float32)).astype(jnp.bfloat16)
        tables += [high, low]
    return np.stack(tables + [-tables[2], -tables[3]])


def split(value):
    high = value.astype(jnp.bfloat16)
    return high, (value - high.astype(jnp.float32)).astype(jnp.bfloat16)


def mul(left, right):
    return jnp.dot(left, right, preferred_element_type=jnp.float32)


def left_product(high, low, value):
    first, second = split(value)
    return mul(high, first) + (mul(high, second) + mul(low, first))


def right_product(value, high, low):
    first, second = split(value)
    return mul(first, high) + (mul(second, high) + mul(first, low))


def lanes(shape):
    return lax.broadcasted_iota(jnp.int32, shape, 1)


def pack(real, imag):
    half = real.shape[1] // 2
    first = lanes(real.shape) < half
    low = jnp.where(first, real, pltpu.roll(imag, half, 1))
    high = jnp.where(first, pltpu.roll(real, half, 1), imag)
    return low, high


def unpack(low, high):
    half = low.shape[1] // 2
    first = lanes(low.shape) < half
    real = jnp.where(first, low, pltpu.roll(high, half, 1))
    imag = jnp.where(first, pltpu.roll(low, half, 1), high)
    return real, imag


def grow_rows(term, skew):
    count, width = term.shape
    tiles = count // TILE
    sub = lax.broadcasted_iota(jnp.int32, (tiles, TILE, width), 1)
    turned = pltpu.roll(term.reshape(tiles, TILE, width), skew, 1)
    late = jnp.where(sub < skew, turned, 0.0)
    soon = jnp.where(sub < skew, 0.0, turned)
    blank = jnp.zeros((1, TILE, width), jnp.float32)
    grown = jnp.concatenate([soon, blank], 0) + jnp.concatenate([blank, late], 0)
    return grown.reshape(count + TILE, width)


def lane_turn(col, width):
    return jnp.where(col < 0, col + width, col)


class Plain:
    def __init__(self, value):
        self.value = value

    def __getitem__(self, where):
        row, col = where
        return self.value[row, col]


class Spot:
    def __init__(self):
        row, col = lax.axis_index("row"), lax.axis_index("col")
        self.side = lax.rem(col, 2)
        self.odd = self.side != 0
        self.row_side = lax.rem(row, 2)
        self.odd_row = self.row_side != 0
        self.has_above = row != 0
        self.has_below = row != lax.axis_size("row") - 1
        self.has_far = (col != 0) & (col != lax.axis_size("col") - 1)


def first_kernel(tile, offsets, counts, first, second, meta, offsets_here, counts_here, sems):
    spot = Spot()
    side = tile.shape[1]
    steps, _, slots = offsets.shape
    near_edge = pl.multiple_of(spot.row_side * RIM, RIM)
    copies = [
        pltpu.make_async_copy(offsets, offsets_here, sems.at[0]),
        pltpu.make_async_copy(counts, counts_here, sems.at[1]),
    ]
    for part in range(2):
        rows = pl.ds(part * RIM, RIM)
        lower = pl.ds(side - RIM - near_edge, RIM)
        upper = pl.ds(near_edge, RIM)
        copies.append(pltpu.make_async_copy(tile.at[part, lower], first.at[rows], sems.at[2 + part]))
        copies.append(pltpu.make_async_copy(tile.at[part, upper], second.at[rows], sems.at[4 + part]))
    for copy in copies:
        copy.start()
    meta[...] = jnp.zeros_like(meta)
    for copy in copies[:2]:
        copy.wait()
    for step in range(steps):
        meta[3 * step : 3 * step + 2, :slots] = offsets_here[step].astype(jnp.float32)
        count = counts_here[:, step : step + 1].astype(jnp.float32)
        meta[3 * step + 2 : 3 * step + 3] = jnp.broadcast_to(count, (1, meta.shape[1]))
    first[2 * RIM :] = meta[...]
    second[2 * RIM :] = meta[...]
    for copy in copies[2:]:
        copy.wait()


def early_kernel(tile, meta, first, far):
    odd = Spot().odd
    side = tile.shape[1]
    for at, real, imag in ((0, first[:RIM], first[RIM : 2 * RIM]), (RIM, tile[0], tile[1])):
        low, high = pack(real, imag)
        far[at : at + low.shape[0]] = jnp.where(odd, high, low)
    far[RIM + side : RIM + side + TILE] = first[2 * RIM :]
    far[RIM + side + TILE :] = meta[...]


def strips_kernel(tile, meta, first, second, tall, near, far):
    side = tile.shape[1]
    spot = Spot()
    odd, odd_row = spot.odd, spot.odd_row
    above = jnp.where(spot.has_above, jnp.where(odd_row, first[...], second[...]), 0.0)
    below = jnp.where(spot.has_below, jnp.where(odd_row, second[...], first[...]), 0.0)
    for part in range(2):
        tall[part, :RIM] = above[part * RIM : (part + 1) * RIM]
        tall[part, RIM : RIM + side] = tile[part]
        tall[part, RIM + side :] = below[part * RIM : (part + 1) * RIM]
    low, high = pack(tall[0], tall[1])
    rows = low.shape[0]
    near[:rows] = jnp.where(odd, low, high)
    near[rows : rows + TILE] = above[2 * RIM :]
    near[rows + TILE : rows + 2 * TILE] = meta[...]
    near[rows + 2 * TILE :] = below[2 * RIM :]
    out = jnp.where(odd, high, low)
    far[:RIM] = jnp.where(odd_row, out[RIM + side :], out[:RIM])
    far[RIM:] = jnp.where(odd_row, below[2 * RIM :], above[2 * RIM :])


def window_place(starts, step, slot, width):
    row = starts[3 * step, slot] + RIM
    col = starts[3 * step + 1, slot]
    base = pl.multiple_of(row // TILE * TILE, TILE)
    lane = lanes((width + TILE, width))
    outside = (lane < col) | (lane >= width + col)
    return pl.ds(base, width + TILE), row - base, col, outside


def take_windows(starts, field, wins, weight, step):
    slots, _, width, _ = wins.shape
    tiles = width // TILE
    sub = lax.broadcasted_iota(jnp.int32, (tiles, TILE, width), 1)
    total = None
    for slot in range(slots):
        rows, skew, col, outside = window_place(starts, step, slot, width)
        live = jnp.where(slot < starts[3 * step + 2, 0], 1.0, 0.0).astype(jnp.float32)
        lift = jnp.where(skew > 0, TILE - skew, 0)
        back = lane_turn(-col, width)
        power = None
        for part in range(2):
            mixed = jnp.where(outside, field[part, rows, width:], field[part, rows, :width])
            turned = pltpu.roll(mixed.reshape(tiles + 1, TILE, width), lift, 1)
            lined = jnp.where(sub < TILE - skew, turned[:-1], turned[1:])
            win = pltpu.roll(lined.reshape(width, width), back, 1)
            wins[slot, part] = win
            power = win * win if power is None else power + win * win
        total = power * live if total is None else total + power * live
    weight[...] = total


def field_kernel(scan, tall, near, far, wins, weight, field, *, step):
    spot = Spot()
    width = tall.shape[2]
    rows = tall.shape[1]
    from_near, from_far = near[:rows], jnp.where(spot.has_far, far[:rows], 0.0)
    sides = unpack(
        jnp.where(spot.odd, from_far, from_near), jnp.where(spot.odd, from_near, from_far)
    )
    for part in range(2):
        field[part, :rows, :width] = tall[part]
        field[part, :rows, width:] = sides[part]
        field[part, rows:] = jnp.zeros_like(field[part, rows:])
    starts = Plain(scan[...])
    take_windows(starts, field, wins, weight, step)


def slots_kernel(
    scan, wins, win_weight, probe, amps, tables,
    core_out, far_out, keep_out, sums_out, sums, totals, psis, *, step,
):
    starts = Plain(scan[...])
    spot = Spot()
    width = probe.shape[1]
    rows_all = sums_out.shape[1]
    slots = amps.shape[0]
    odd = spot.odd
    sums[...] = jnp.zeros_like(sums)
    cos_h, cos_l, sin_h, sin_l, neg_h, neg_l = (tables[k] for k in range(6))

    def square(left_up, right_up, left_down, right_down):
        upper = jnp.concatenate([left_up, right_up], 1)
        return jnp.concatenate([upper, jnp.concatenate([left_down, right_down], 1)], 0)

    full_h, full_l = square(cos_h, neg_h, sin_h, cos_h), square(cos_l, neg_l, sin_l, cos_l)
    flip_h, flip_l = square(cos_h, sin_h, neg_h, cos_h), square(cos_l, sin_l, neg_l, cos_l)
    pro_r, pro_i = probe[0], probe[1]
    columns = []
    for slot in range(slots):
        psi_r = pro_r * wins[slot, 0] - pro_i * wins[slot, 1]
        psi_i = pro_r * wins[slot, 1] + pro_i * wins[slot, 0]
        psis[slot, 0] = psi_r
        psis[slot, 1] = psi_i
        columns.append(jnp.concatenate([psi_r, psi_i], 0))

    def block(value, k):
        return value[k * width : (k + 1) * width]

    def turn(half):
        parts = []
        for k in range(slots):
            both = half[:, k * width : (k + 1) * width]
            parts.append(jnp.concatenate([both[:width], both[width:]], 1))
        return jnp.concatenate(parts, 0)

    half = left_product(full_h, full_l, jnp.concatenate(columns, 1))
    wave = right_product(turn(half), flip_h, flip_l)
    columns = []
    for slot in range(slots):
        far_r, far_i = block(wave, slot)[:, :width], block(wave, slot)[:, width:]
        factor = amps[slot] * lax.rsqrt(jnp.maximum(far_r * far_r + far_i * far_i, 1.0))
        columns.append(jnp.concatenate([far_r * factor, far_i * factor], 0))
    half = left_product(flip_h, flip_l, jnp.concatenate(columns, 1))
    wave = right_product(turn(half), full_h, full_l)
    total = None
    for slot in range(slots):
        rows, skew, col, outside = window_place(starts, step, slot, width)
        ahead = lane_turn(col, width)
        live = jnp.where(slot < starts[3 * step + 2, 0], 1.0, 0.0).astype(jnp.float32)
        win_r, win_i = wins[slot, 0], wins[slot, 1]
        chi_r = (block(wave, slot)[:, :width] - psis[slot, 0]) * live
        chi_i = (block(wave, slot)[:, width:] - psis[slot, 1]) * live

        def deposit(part, term):
            grown = grow_rows(pltpu.roll(term, ahead, 1), skew)
            sums[part, rows, :width] += jnp.where(outside, 0.0, grown)
            sums[part, rows, width:] += jnp.where(outside, grown, 0.0)

        deposit(0, pro_r * chi_r + pro_i * chi_i)
        deposit(1, pro_r * chi_i - pro_i * chi_r)
        terms = (win_r * chi_r + win_i * chi_i, win_r * chi_i - win_i * chi_r)
        total = terms if total is None else tuple(a + b for a, b in zip(total, terms))
    half = width // 2
    totals[0], totals[1], totals[2] = total[0], total[1], win_weight[...]
    kept = pl.ds(pl.multiple_of(spot.side * half, half), half)
    given = pl.ds(pl.multiple_of((1 - spot.side) * half, half), half)
    for part in range(3):
        keep_out[part * half : (part + 1) * half] = totals[part, kept]
        core_out[part * half : (part + 1) * half] = totals[part, given]
    for part in range(2):
        sums_out[part] = sums[part, :rows_all, :width]
    low, high = pack(sums[0, :rows_all, width:], sums[1, :rows_all, width:])
    core_out[3 * half :] = jnp.where(odd, high, low)
    far_out[...] = jnp.where(odd, low, high)


def folded(spot, tall, near, far):
    start = near.shape[0] - tall.shape[1]
    odd = spot.odd
    from_near, from_far = near[start:], jnp.where(spot.has_far, far[...], 0.0)
    extra = unpack(jnp.where(odd, from_near, from_far), jnp.where(odd, from_far, from_near))
    return tall[0] + extra[0], tall[1] + extra[1]


def fold_kernel(tall, near, far, first, second):
    rows = first.shape[1]
    spot = Spot()
    odd_row = spot.odd_row
    whole = folded(spot, tall, near, far)
    for part in range(2):
        up, down = whole[part][:rows], whole[part][rows:]
        first[part] = jnp.where(odd_row, up, down)
        second[part] = jnp.where(odd_row, down, up)


def last_fold_kernel(tall, near, far, middle, first, second):
    rows = middle.shape[1]
    spot = Spot()
    odd_row = spot.odd_row
    whole = folded(spot, tall, near, far)
    for part in range(2):
        up, down = whole[part][:RIM], whole[part][RIM + rows :]
        middle[part] = whole[part][RIM : RIM + rows]
        first[part] = jnp.where(odd_row, up, down)
        second[part] = jnp.where(odd_row, down, up)


def weight_kernel(metas, probe, out, spread, *, step, slots):
    width = probe.shape[1]
    lane = lanes((width + TILE, width))
    spread[...] = jnp.zeros_like(spread)
    weight = probe[0] * probe[0] + probe[1] * probe[1]
    for index in range(metas.shape[0]):
        count = metas[index, (3 * step + 2) * slots]
        for slot in range(slots):
            row = metas[index, 3 * step * slots + slot] + (RIM + width + (index // 3 - 1) * width)
            col = metas[index, (3 * step + 1) * slots + slot] + (index % 3 - 1) * width

            base = pl.multiple_of(row // TILE * TILE, TILE)
            grown = grow_rows(pltpu.roll(weight, lax.rem(col + 2 * width, width), 1), row - base)
            edge = jnp.where(slot < count, col, 2 * width)
            inside = (lane >= edge) & (lane < width + edge)
            spread[pl.ds(base, width + TILE)] += jnp.where(inside, grown, 0.0)

    out[...] = spread[width : width + out.shape[0]]


def update_kernel(tall, sent_1, sent_2, got_1, got_2, weight, _, new_tall, near, far):
    rows = sent_1.shape[1]
    spot = Spot()
    odd, odd_row = spot.odd, spot.odd_row
    for part in range(2):
        up = jnp.where(odd_row, sent_1[part], sent_2[part])
        down = jnp.where(odd_row, sent_2[part], sent_1[part])
        above = jnp.where(odd_row, got_1[part], got_2[part])
        below = jnp.where(odd_row, got_2[part], got_1[part])
        up = up + jnp.where(spot.has_above, above, 0.0)
        down = down + jnp.where(spot.has_below, below, 0.0)
        head = tall[part, :rows] + up / (weight[:rows] + EPS)
        tail = tall[part, rows:] + down / (weight[rows:] + EPS)
        new_tall[part, :RIM] = jnp.where(spot.has_above, head[:RIM], 0.0)
        new_tall[part, RIM:rows] = head[RIM:]
        new_tall[part, rows : 2 * rows - RIM] = tail[: rows - RIM]
        new_tall[part, 2 * rows - RIM :] = jnp.where(spot.has_below, tail[rows - RIM :], 0.0)
    low, high = pack(new_tall[0], new_tall[1])
    near[...] = jnp.where(odd, low, high)
    far[...] = jnp.where(odd, high, low)


def last_kernel(tall, middle, got_1, got_2, weight, mine, other, tile, probe):
    side = tile.shape[1]
    half = mine.shape[1]
    spot = Spot()
    odd, odd_row = spot.odd, spot.odd_row
    for part in range(2):
        above = jnp.where(odd_row, got_1[part], got_2[part])
        below = jnp.where(odd_row, got_2[part], got_1[part])
        above = jnp.where(spot.has_above, above, 0.0)
        below = jnp.where(spot.has_below, below, 0.0)
        num = middle[part] + jnp.concatenate([above, below], 0)
        tile[part] = tall[part, RIM : RIM + side] + num / (weight[RIM : RIM + side] + EPS)
        probe[part, :half] = jnp.where(odd, other[part], mine[part])
        probe[part, half:] = jnp.where(odd, mine[part], other[part])


def call(kernel, shapes, places, operands, flops=1000000, moved=MIB, scratch=(), more=(), limit=16):
    vmem = pl.BlockSpec(memory_space=pltpu.VMEM)
    smem = pl.BlockSpec(memory_space=pltpu.SMEM)
    anywhere = pl.BlockSpec(memory_space=pl.ANY)
    return pl.pallas_call(
        kernel,
        out_shape=tuple(jax.ShapeDtypeStruct(shape, jnp.float32) for shape in shapes),
        in_specs=[{"s": smem, "a": anywhere}.get(where, vmem) for where in places.ljust(len(operands), "v")],
        out_specs=tuple(vmem for _ in shapes),
        scratch_shapes=[pltpu.VMEM(shape, jnp.float32) for shape in scratch] + list(more),
        compiler_params=pltpu.CompilerParams(vmem_limit_bytes=limit * MIB),
        cost_estimate=pl.CostEstimate(flops=flops, bytes_accessed=moved, transcendentals=0),
    )(*operands)


def swap(value, axis, bit):
    return lax.ppermute(value, axis, [(i, i ^ bit) for i in range(lax.axis_size(axis))])


def swap_far(value):
    rows, cols = lax.axis_size("row"), lax.axis_size("col")
    pairs = []
    for row in range(rows):
        for col in range(cols):
            to_row, to_col = row, col + (1 if col % 2 else -1)
            if not 0 <= to_col < cols:
                to_row, to_col = row ^ 1, col
            pairs.append((row * cols + col, to_row * cols + to_col))
    return lax.ppermute(value, AXES, pairs)


def swap_rows(value):
    rows, cols = lax.axis_size("row"), lax.axis_size("col")
    pairs = []
    for row in range(rows):
        for col in range(cols):
            to_row, to_col = row + (1 if row % 2 else -1), col
            if not 0 <= to_row < rows:
                to_row, to_col = row, col ^ 1
            pairs.append((row * cols + col, to_row * cols + to_col))
    return lax.ppermute(value, AXES, pairs)


def after(*values):
    return lax.optimization_barrier(values)


def chip_steps():
    steps = [("row", 1)]
    for axis in ("col", "row"):
        bit = 2
        while bit < lax.axis_size(axis):
            steps.append((axis, bit))
            bit *= 2
    return steps


def swap_both(value):
    rows, cols = lax.axis_size("row"), lax.axis_size("col")
    pairs = [(r * cols + c, (r ^ 1) * cols + (c ^ 2)) for r in range(rows) for c in range(cols)]
    return lax.ppermute(value, AXES, pairs)


def add_plane(part, weight):
    part_y, part_x, part_xy = swap(part, "row", 1), swap(part, "col", 2), swap_both(part)
    if weight is not None:
        part_xy, weight = after(part_xy, weight)
    return (part + part_y) + (part_x + part_xy)


def add_step(part, step):
    return part + swap(part, *step)


def body(object_field, probe, positions, counts, amplitude):
    side = object_field.shape[1]
    width = probe.shape[1]
    half = width // 2
    steps = positions.shape[2]
    slots = positions.shape[3]
    tall_rows = side + 2 * RIM
    row, col = lax.axis_index("row"), lax.axis_index("col")
    odd, odd_row = col % 2, row % 2
    outer = (col == 0) | (col == lax.axis_size("col") - 1)
    tables = jnp.asarray(dft_tables(width))

    offsets = jnp.swapaxes(positions[0, 0], 1, 2)
    flat = 2 * RIM
    first, second, meta = call(
        first_kernel,
        ((flat + TILE, width), (flat + TILE, width), (TILE, width)),
        "aaa",
        (object_field, offsets, counts[0]),
        more=(
            pltpu.VMEM(offsets.shape, jnp.int32),
            pltpu.VMEM((1, steps), jnp.int32),
            pltpu.SemaphoreType.DMA((6,)),
        ),
        limit=60,
    )
    scan = meta[: 3 * steps, :slots].astype(jnp.int32)
    first, second = swap(first, "row", 1), swap_rows(second)
    (early,) = call(
        early_kernel,
        ((RIM + side + 2 * TILE, width),),
        "",
        (object_field, meta, first),
    )
    early = swap_far(early)
    tall, near, late = call(
        strips_kernel,
        ((2, tall_rows, side), (tall_rows + 3 * TILE, width), (RIM + TILE, width)),
        "",
        (object_field, meta, first, second),
    )
    near, late = swap(near, "col", 1), swap_far(late)
    turned = odd_row != 0
    sides = early[:RIM], late[:RIM]
    ends = early[RIM + side : RIM + side + TILE], late[RIM:]
    far = jnp.concatenate(
        [
            jnp.where(turned, sides[0], sides[1]),
            early[RIM : RIM + side],
            jnp.where(turned, sides[1], sides[0]),
            jnp.where(turned, ends[0], ends[1]),
            early[RIM + side + TILE :],
            jnp.where(turned, ends[1], ends[0]),
        ],
        0,
    )

    def three(value):
        return value[tall_rows:].reshape(3, TILE, width)[:, : 3 * steps, :slots]

    above = jnp.where(row > 0, jnp.where(odd_row != 0, first[flat:], second[flat:]), 0.0)
    below = jnp.where(row < lax.axis_size("row") - 1, jnp.where(odd_row != 0, second[flat:], first[flat:]), 0.0)
    here = jnp.stack([above, meta, below])[:, : 3 * steps, :slots]
    sides = three(near), jnp.where(outer, 0.0, three(far))
    left = jnp.where(odd != 0, sides[0], sides[1])
    right = jnp.where(odd != 0, sides[1], sides[0])
    metas = jnp.stack([left, here, right], 1).reshape(9, -1).astype(jnp.int32)

    def windows(step, tall, near, far):
        return call(
            functools.partial(field_kernel, step=step),
            ((slots, 2, width, width), (width, width)),
            "",
            (scan, tall, near, far),
            scratch=((2, tall_rows + TILE, 2 * width),),
        )

    wins, win_weight = windows(0, tall, near, far)
    current = probe
    for step in range(steps):
        last = step == steps - 1
        core, out_far, kept, sums = call(
            functools.partial(slots_kernel, step=step),
            (
                (3 * half + tall_rows, width),
                (tall_rows, width),
                (3 * half, width),
                (2, tall_rows, width),
            ),
            "",
            (scan, wins, win_weight, current, amplitude[0, 0, step], tables),
            flops=slots * 96 * width * width * width,
            moved=4 * MIB,
            scratch=(
                (2, tall_rows + TILE, 2 * width),
                (3, width, width),
                (slots, 2, width, width),
            ),
            limit=24,
        )
        core = swap(core, "col", 1)
        out_far = swap_far(out_far)
        (weight,) = call(
            functools.partial(weight_kernel, step=step, slots=slots),
            ((tall_rows, width),),
            "s",
            (metas, current),
            scratch=((tall_rows + 2 * width + TILE, width),),
            moved=8 * MIB,
        )
        part = kept + core[: 3 * half]
        if last:
            middle, sent_1, sent_2 = call(
                last_fold_kernel,
                ((2, side, width), (2, RIM, width), (2, RIM, width)),
                "",
                (sums, core, out_far),
                moved=16 * MIB,
            )
            got_1, got_2 = swap(sent_1, "row", 1), swap_rows(sent_2)
            part = add_plane(part, weight)
            for other_step in chip_steps()[2:-1]:
                part = add_step(part, other_step)
            part = add_step(part, chip_steps()[-1])
        else:
            sent_1, sent_2 = call(
                fold_kernel,
                ((2, tall_rows // 2, width), (2, tall_rows // 2, width)),
                "",
                (sums, core, out_far),
            )
            got_1, got_2 = swap(sent_1, "row", 1), swap_rows(sent_2)
            part = add_plane(part, weight)
            for other_step in chip_steps()[2:-1]:
                part = add_step(part, other_step)
            tall, near, far = call(
                update_kernel,
                ((2, tall_rows, side), (tall_rows, width), (tall_rows, width)),
                "",
                (tall, sent_1, sent_2, got_1, got_2, weight, part[:TILE]),
                moved=8 * MIB,
            )
            near = swap(near, "col", 1)
            far_1, far_2 = swap_far(far[: tall_rows // 2]), swap_far(far[tall_rows // 2 :])
            part = add_step(part, chip_steps()[-1])
            far = jnp.concatenate([far_1, far_2], 0)
            wins, win_weight = windows(step + 1, tall, near, far)
        mine = lax.dynamic_slice_in_dim(current, odd * half, half, 1)
        part = part.reshape(3, half, width)
        mine = mine + part[:2] / (part[2] + EPS)[None]
        other = swap(mine, "col", 1)
        if last:
            return call(
                last_kernel,
                ((2, side, side), (2, width, width)),
                "",
                (tall, middle, got_1, got_2, weight, mine, other),
                moved=4 * MIB,
            )
        low = jnp.where(odd == 0, mine, other)
        high = jnp.where(odd == 0, other, mine)
        current = jnp.concatenate([low, high], 1)


def solution(mesh):
    return jax.shard_map(
        body,
        mesh=mesh,
        in_specs=(
            P(None, "row", "col"),
            P(),
            P("row", "col", None, None, None),
            P("row", "col", None),
            P("row", "col", None, None, None, None),
        ),
        out_specs=(P(None, "row", "col"), P()),
        check_vma=False,
    )
```
